32 devices in a mesh: sub: 8 (over z, y), freq: 4 (over x, core).
Axes of the slice: x: 2, y: 2, z: 4, core: 2. Of those that a mesh axis runs over, the one named last changes fastest.
Arguments:
- response: bfloat16 [4, 96, 96, 256], P('freq', 'sub'), may hold values from -6 to 6
- measured: bfloat16 [4, 768, 256], P('freq', 'sub'), may hold values from -6 to 6
- sensor_owner: int32 [768], P('sub'), may hold values from 0 to 7, as said below
- sensor_row: int32 [768], P('sub'), may hold values from 0 to 1151
- adj_diag: bfloat16 [4, 96, 2, 96, 96], P('freq', 'sub')
- adj_off: bfloat16 [4, 96, 5, 2, 96, 96], P('freq', 'sub')
- block_cols: int32 [96, 5], P('sub'), may hold values from 0 to 13, as said below
- precond: bfloat16 [4, 96, 2, 96, 96], P('freq', 'sub')
- stiff_deriv: bfloat16 [96, 96, 96], P('sub'), may hold values from -0.625 to 0.625
Outputs:
- adjoint: bfloat16 [4, 96, 96, 256], P('freq', 'sub')
- gradient: float32 [96], P('sub')
The draws below stay inside these ranges and needn't reach their ends.
Inputs may be any that keep to these rules, and one draw needn't show every extreme that they name: `sensor_owner`: among the 96 channels held by one index of sub, no subdomain is named more than 36 times, and one subdomain is named exactly 36 times by the channels of every index of sub. `block_cols`: in every subdomain some block row has a coupling tile with column 0 and some has one with column 13.
All inputs are finite; a program needn't handle non-finite values.
Results may differ from the reference program's by a relative error of at most 0.0061.
Values may be sent and summed in bfloat16 or wider, within the bound.
A program may use at most 64 MiB of HBM per device.

```python
import math
import jax
import jax.numpy as jnp
from jax import lax

BS = 96
R = 128
NBD = 12
NNB = 5
SWEEPS = 3
SENS_DEV = 96
FREQ = 4
NB = 96
NSENS = 768
CAP = 36


def tile_noise(rng_key, shape):
    return jax.random.normal(rng_key, shape, jnp.float32)


def diag_level(rng_key):
    return jax.random.uniform(jax.random.fold_in(rng_key, 11), (FREQ, NB, BS), jnp.float32, 2.0, 4.0)


def draw_adj_diag(key, part):
    level = diag_level(key)
    noise = tile_noise(jax.random.fold_in(key, 12), (FREQ, NB, 2, BS, BS))
    identity = jnp.eye(BS, dtype=jnp.float32)
    real_part = noise[:, :, 0] * (1.0 / math.sqrt(BS)) + level[..., None] * identity
    imag_part = noise[:, :, 1] * (0.5 / math.sqrt(BS)) + 0.4 * identity
    return jnp.stack([real_part, imag_part], axis=2).astype(jnp.bfloat16)


def draw_precond(key, part):
    level = diag_level(key)
    noise = tile_noise(jax.random.fold_in(key, 13), (FREQ, NB, 2, BS, BS))
    identity = jnp.eye(BS, dtype=jnp.float32)
    denominator = level * level + 0.16
    real_part = (level / denominator)[..., None] * identity + noise[:, :, 0] * (0.1 / math.sqrt(BS))
    imag_part = (-0.4 / denominator)[..., None] * identity + noise[:, :, 1] * (0.05 / math.sqrt(BS))
    return jnp.stack([real_part, imag_part], axis=2).astype(jnp.bfloat16)


def draw_adj_off(key, part):
    noise = tile_noise(jax.random.fold_in(key, 14), (FREQ, NB, NNB, 2, BS, BS))
    factors = jnp.array([0.5, 0.25], jnp.float32)[:, None, None] * (1.0 / math.sqrt(BS))
    return (noise * factors).astype(jnp.bfloat16)


def draw_block_cols(key, part):
    subdomain_count = NB // NBD
    columns = jax.random.randint(jax.random.fold_in(key, 15), (subdomain_count, NBD, NNB), 0, NBD + 2, jnp.int32)
    columns = columns.at[:, 0, 0].set(0)
    columns = columns.at[:, NBD - 1, 0].set(NBD + 1)
    return columns.reshape(NB, NNB)


def draw_sensor_owner(key, part):
    subdomain_count = NSENS // SENS_DEV
    hot_owner = jax.random.randint(jax.random.fold_in(key, 16), (), 0, subdomain_count, jnp.int32)
    offsets = jax.random.randint(jax.random.fold_in(key, 17), (subdomain_count, 1), 0, subdomain_count - 1, jnp.int32)
    positions = jnp.arange(SENS_DEV, dtype=jnp.int32)[None, :]
    spread = (positions - CAP + offsets) % (subdomain_count - 1)
    owners = jnp.where(positions < CAP, hot_owner, (hot_owner + 1 + spread) % subdomain_count)
    perm_keys = jax.random.split(jax.random.fold_in(key, 18), subdomain_count)
    orders = jax.vmap(lambda perm_key: jax.random.permutation(perm_key, SENS_DEV))(perm_keys)
    owners = jnp.take_along_axis(owners, orders.astype(jnp.int32), axis=1)
    return owners.reshape(NSENS).astype(jnp.int32)


def plant(drawn, stream_key, low, top_value):
    longest = drawn.shape.index(max(drawn.shape))
    spots = []
    for shift in (0, 1):
        where = [jax.random.randint(jax.random.fold_in(stream_key, axis), (), 0, length) for axis, length in enumerate(drawn.shape)]
        where[longest] = (where[longest] + shift) % drawn.shape[longest]
        spots.append(tuple(where))
    return drawn.at[spots[0]].set(low).at[spots[1]].set(top_value)


def shard_levels(own_key, shape, cuts, least, largest):
    def one(axis_at, blocks):
        heights = jax.random.uniform(jax.random.fold_in(jax.random.fold_in(own_key, 6), axis_at), (blocks,), jnp.float32, least / len(cuts), largest / len(cuts))
        return jnp.repeat(jnp.exp(heights), shape[axis_at] // blocks).reshape((-1,) + (1,) * (len(shape) - axis_at - 1))

    factor_of = one(*cuts[0])
    for cut in cuts[1:]:
        factor_of = factor_of * one(*cut)
    return factor_of


def bell_draw(stream_key, shape, scale, reach, pieces=(), kind=jnp.bfloat16):
    values = jax.random.normal(stream_key, shape, jnp.float32) * scale
    if len(pieces) > 0:
        values = shard_levels(stream_key, shape, pieces, -0.22, 0.18) * values
    return jnp.clip(values, min=-reach, max=reach).astype(kind)


def setup_inputs(seed: int = 0) -> dict:
    key_of = jax.random.split(jax.random.key(seed), 10)
    return {
        "response": bell_draw(key_of[0], (FREQ, NB, BS, 2 * R), 1.0, 6.0, ((0, 4), (1, 8))),
        "measured": bell_draw(key_of[1], (FREQ, NSENS, 2 * R), 1.0, 6.0, ((0, 4), (1, 8))),
        "sensor_owner": draw_sensor_owner(jax.random.fold_in(key_of[9], 71), 0),
        "sensor_row": plant(jax.random.randint(key_of[3], (NSENS,), 0, NBD * BS), jax.random.fold_in(key_of[3], 1), 0, (NBD * BS) - 1).astype(jnp.int32),
        "adj_diag": draw_adj_diag(jax.random.fold_in(key_of[9], 71), 0),
        "adj_off": draw_adj_off(jax.random.fold_in(key_of[9], 71), 0),
        "block_cols": draw_block_cols(jax.random.fold_in(key_of[9], 71), 0),
        "precond": draw_precond(jax.random.fold_in(key_of[9], 71), 0),
        "stiff_deriv": bell_draw(key_of[8], (NB, BS, BS), BS ** -0.5, 0.625, ((0, 8),)),
    }


def complex_apply(tile_set, vectors):
    column_half = vectors.shape[-1] // 2
    real_part = jnp.einsum('bij,bjn->bin', tile_set[:, 0], vectors, precision=lax.Precision.HIGHEST)
    imag_part = jnp.einsum('bij,bjn->bin', tile_set[:, 1], vectors, precision=lax.Precision.HIGHEST)
    return jnp.concatenate([real_part[..., :column_half] - imag_part[..., column_half:], real_part[..., column_half:] + imag_part[..., :column_half]], axis=-1)

def coupled_apply(iterate, off_tiles, padded_index):
    subdomain_count = NB // NBD
    col_count = iterate.shape[-1]
    column_half = col_count // 2
    empty_zero_block = jnp.zeros((1, BS, col_count), jnp.bfloat16)
    padded = jnp.concatenate([empty_zero_block, iterate, empty_zero_block], axis=0)

    def per_sub(inputs_pair):
        tile_set, index_set = inputs_pair
        near_blocks = padded[index_set].astype(jnp.float32)
        tile_f32 = tile_set.astype(jnp.float32)
        real_part = jnp.einsum('bkij,bkjn->bin', tile_f32[:, :, 0], near_blocks, precision=lax.Precision.HIGHEST)
        imag_part = jnp.einsum('bkij,bkjn->bin', tile_f32[:, :, 1], near_blocks, precision=lax.Precision.HIGHEST)
        return jnp.concatenate([real_part[..., :column_half] - imag_part[..., column_half:], real_part[..., column_half:] + imag_part[..., :column_half]], axis=-1)
    result = lax.map(per_sub, (off_tiles.reshape(subdomain_count, NBD, NNB, 2, BS, BS), padded_index.reshape(subdomain_count, NBD, NNB)))
    return result.reshape(NB, BS, col_count)

def reference(response, measured, sensor_owner, sensor_row, adj_diag, adj_off, block_cols, precond, stiff_deriv):
    col_count = 2 * R
    flat_index = (sensor_owner * (NBD * BS) + sensor_row).astype(jnp.int32)
    leading_block = jnp.arange(NB, dtype=jnp.int32) // NBD * NBD
    padded_index = (leading_block[:, None] + block_cols).astype(jnp.int32)
    grad_scale = 1.0 / math.sqrt(2 * BS * R)
    stiff_f32 = stiff_deriv.astype(jnp.float32)
    adjoints = []
    gradient = jnp.zeros((NB,), jnp.float32)
    for freq_step in range(FREQ):
        resp_now = response[freq_step]
        flat_resp = resp_now.reshape(NB * BS, col_count).astype(jnp.float32)
        misfit = flat_resp[flat_index] - measured[freq_step].astype(jnp.float32)
        load_rhs = jnp.zeros((NB * BS, col_count), jnp.float32).at[flat_index].add(misfit).reshape(NB, BS, col_count)
        diag_f32 = adj_diag[freq_step].astype(jnp.float32)
        prec_f32 = precond[freq_step].astype(jnp.float32)
        load_low = lax.optimization_barrier(load_rhs.astype(jnp.bfloat16)).astype(jnp.float32)
        adjoint = complex_apply(prec_f32, load_low)
        for jacobi_sweep_step in range(SWEEPS - 1):
            iterate = lax.optimization_barrier(adjoint.astype(jnp.bfloat16))
            applied = complex_apply(diag_f32, iterate.astype(jnp.float32)) + coupled_apply(iterate, adj_off[freq_step], padded_index)
            update = lax.optimization_barrier((load_rhs - applied).astype(jnp.bfloat16)).astype(jnp.float32)
            adjoint = adjoint + complex_apply(prec_f32, update)
        adjoints.append(adjoint.astype(jnp.bfloat16))
        stiff_resp = jnp.einsum('bij,bjn->bin', stiff_f32, resp_now.astype(jnp.float32), precision=lax.Precision.HIGHEST)
        gradient = gradient + lax.optimization_barrier(jnp.sum(adjoint * stiff_resp, axis=(1, 2))) * grad_scale
    return (jnp.stack(adjoints), gradient)
```

```python
import functools
import math

import jax
import jax.numpy as jnp
from jax import lax
from jax.experimental import pallas as pl
from jax.experimental.pallas import tpu as pltpu
from jax.sharding import PartitionSpec as P

MESH = pl.DeviceIdType.MESH
F32 = jnp.float32
BF16 = jnp.bfloat16
SWEEPS = 3
LANES = 128
CAPS = {8: 36, 128: 3}


def round_up(value, unit):
    return -(-value // unit) * unit


def iota(shape, dim):
    return lax.broadcasted_iota(jnp.int32, shape, dim)


def one_hot(mask):
    return jnp.where(mask, 1.0, 0.0).astype(BF16)


def dot(a, b):
    return jnp.dot(a, b, preferred_element_type=F32)


def combine(prod):
    rows, half = prod.shape[0] // 2, prod.shape[1] // 2
    left = prod[:rows, :half] - prod[rows:, half:]
    right = prod[:rows, half:] + prod[rows:, :half]
    return jnp.concatenate([left, right], axis=1)


def kernel(
    n_sub, n_freq, slots, group,
    resp_hbm, meas, owner, row, diag_hbm, off_hbm, cols, prec_hbm, stiff_hbm,
    out, grad,
    resp, diag, off, prec, stiff, tiles, ext_0, ext_1, load, lam, stiff_resp, scat,
    idx_send, idx_recv, pack_send, pack_recv, meas_all, part, part_recv,
    in_sem, idx_ss, idx_rs, pack_ss, pack_rs, halo_ss, halo_rs, part_ss, part_rs,
):
    nb, bs, width = resp.shape
    nnb = off.shape[1]
    half = width // 2
    ext = (ext_0, ext_1)
    chans = meas.shape[0]
    lanes = scat.shape[2]
    me = lax.axis_index("sub")
    fr = lax.axis_index("freq")

    loads = [
        pltpu.make_async_copy(src, dst, in_sem.at[i])
        for i, (src, dst) in enumerate(
            [(resp_hbm, resp), (stiff_hbm, stiff), (diag_hbm, diag), (off_hbm, off), (prec_hbm, prec)]
        )
    ]
    for copy in loads:
        copy.start()

    barrier = pltpu.get_barrier_semaphore()
    for j in range(1, n_sub):
        pl.semaphore_signal(barrier, inc=1, device_id={"sub": lax.rem(me + j, n_sub)}, device_id_type=MESH)
    for j in range(1, n_freq):
        pl.semaphore_signal(barrier, inc=1, device_id={"freq": lax.rem(fr + j, n_freq)}, device_id_type=MESH)

    own = owner[...].astype(F32)
    ri, ci = iota((chans, chans), 0), iota((chans, chans), 1)
    own_b = jnp.broadcast_to(own, (chans, chans))
    own_col = jnp.sum(jnp.where(ri == ci, own_b, 0.0), axis=1, keepdims=True)
    same = jnp.where(own_col == own_b, 1.0, 0.0)
    rank = jnp.sum(jnp.where(ri < ci, same, 0.0), axis=0, keepdims=True)
    rank_col = jnp.sum(jnp.where(ci < ri, same, 0.0), axis=1, keepdims=True)
    number = row[...].astype(F32) + 1.0
    high = jnp.floor(number * (1.0 / 64.0))
    low = number - 64.0 * high
    named = iota((n_sub, chans), 0).astype(F32) == own
    digits = jnp.concatenate([jnp.where(named, high, 0.0), jnp.where(named, low, 0.0)], axis=0).astype(BF16)
    shifted = rank_col + (me * slots).astype(F32)
    place = one_hot(iota((chans, lanes), 1).astype(F32) == shifted)
    numbers = dot(digits, place)
    numbers = numbers[:n_sub] * 64.0 + numbers[n_sub:]
    for d in range(n_sub):
        idx_send[d] = numbers[d : d + 1]
    slot = own * float(slots) + rank
    select = one_hot(iota((n_sub * slots, chans), 0).astype(F32) == slot)
    packed = dot(select, meas[...])
    for d in range(n_sub):
        rows = packed[d * slots : (d + 1) * slots]
        pack_send[d] = jnp.concatenate([rows[:, :half], rows[:, half:]], axis=0).astype(BF16)

    pl.semaphore_wait(barrier, n_sub - 1 + n_freq - 1)

    def idx_copy(j):
        dest = lax.rem(me + j, n_sub)
        return pltpu.make_async_remote_copy(
            src_ref=idx_send.at[dest], dst_ref=idx_recv.at[me],
            send_sem=idx_ss.at[dest], recv_sem=idx_rs.at[me],
            device_id={"sub": dest}, device_id_type=MESH,
        )

    def pack_copy(j):
        dest = lax.rem(me + j, n_sub)
        return pltpu.make_async_remote_copy(
            src_ref=pack_send.at[dest], dst_ref=pack_recv.at[me],
            send_sem=pack_ss.at[dest], recv_sem=pack_rs.at[me],
            device_id={"sub": dest}, device_id_type=MESH,
        )

    far_first = sorted(range(1, n_sub), key=lambda j: abs(j - n_sub // 2))
    for j in far_first:
        idx_copy(j).start()
    for j in far_first:
        pack_copy(j).start()
    idx_recv[me] = idx_send[me]
    pack_recv[me] = pack_send[me]

    pad = ext_0.shape[1] - bs
    for buf in ext:
        buf[:, bs:, :] = jnp.zeros((nb + 2, pad, width), BF16)
    used = n_sub * slots
    if lanes > used:
        meas_all[used:, :] = jnp.zeros((lanes - used, width), F32)
    part[...] = jnp.zeros(part.shape, F32)

    @pl.when(me == 0)
    def _():
        for buf in ext:
            buf[0, :bs, :] = jnp.zeros((bs, width), BF16)

    @pl.when(me == n_sub - 1)
    def _():
        for buf in ext:
            buf[nb + 1, :bs, :] = jnp.zeros((bs, width), BF16)

    loads[0].wait()
    loads[1].wait()

    @pl.loop(0, nb // 4)
    def _(g):
        for i in range(4):
            b = g * 4 + i
            stiff_resp[b] = dot(stiff[b], resp[b])

    loads[2].wait()
    loads[3].wait()
    blank = jnp.zeros((2 * bs, LANES - bs), BF16)

    @pl.loop(0, nb)
    def _(b):
        tiles[b, :, :LANES] = jnp.concatenate([diag[b], blank], axis=1)
        for k in range(nnb):
            tiles[b, :, (k + 1) * LANES : (k + 2) * LANES] = jnp.concatenate([off[b, k], blank], axis=1)

    for j in range(1, n_sub):
        source = lax.rem(me + n_sub - j, n_sub)
        pltpu.make_async_remote_copy(
            src_ref=idx_send.at[source], dst_ref=idx_recv.at[source],
            send_sem=idx_ss.at[source], recv_sem=idx_rs.at[source],
            device_id={"sub": source}, device_id_type=MESH,
        ).wait_recv()
    numbers = idx_recv[0]
    for p in range(1, n_sub):
        numbers = numbers + idx_recv[p]
    numbers = jnp.broadcast_to(numbers - 1.0, (bs, lanes))

    @pl.loop(0, nb // 2)
    def _(g):
        for i in range(2):
            b = g * 2 + i
            here = iota((bs, lanes), 0).astype(F32) + (b * bs).astype(F32)
            hit = jnp.where(numbers == here, 1.0, 0.0)
            scat[b] = hit.astype(BF16)
            load[b] = jnp.sum(hit, axis=1, keepdims=True) * resp[b].astype(F32)

    loads[4].wait()
    for j in range(1, n_sub):
        source = lax.rem(me + n_sub - j, n_sub)
        pltpu.make_async_remote_copy(
            src_ref=pack_send.at[source], dst_ref=pack_recv.at[source],
            send_sem=pack_ss.at[source], recv_sem=pack_rs.at[source],
            device_id={"sub": source}, device_id_type=MESH,
        ).wait_recv()
    for p in range(n_sub):
        rows = pack_recv[p].astype(F32)
        meas_all[p * slots : (p + 1) * slots, :] = jnp.concatenate([rows[:slots], rows[slots:]], axis=1)
    rows_in = meas_all[...].astype(BF16)

    def halo(step, low):
        src = ext[step].at[1 if low else nb, pl.ds(0, bs)]
        dst = ext[step].at[nb + 1 if low else 0, pl.ds(0, bs)]
        target = lax.rem(me + (n_sub - 1 if low else 1), n_sub)
        way = 0 if low else 1
        return pltpu.make_async_remote_copy(
            src_ref=src, dst_ref=dst, send_sem=halo_ss.at[step, way], recv_sem=halo_rs.at[step, way],
            device_id={"sub": target}, device_id_type=MESH,
        )

    def halo_start(step):
        @pl.when(me > 0)
        def _():
            halo(step, True).start()

        @pl.when(me < n_sub - 1)
        def _():
            halo(step, False).start()

    def halo_wait(step):
        @pl.when(me > 0)
        def _():
            halo(step, False).wait_recv()

        @pl.when(me < n_sub - 1)
        def _():
            halo(step, True).wait_recv()

    def first(blocks):
        rhs = [load[b] - dot(scat[b], rows_in) for b in blocks]
        for b, value in zip(blocks, rhs):
            load[b] = value
        new = [combine(dot(prec[b], value.astype(BF16))) for b, value in zip(blocks, rhs)]
        for b, value in zip(blocks, new):
            lam[b] = value
            ext_0[b + 1, :bs, :] = value.astype(BF16)

    def sweep(step, blocks):
        updates = []
        for b in blocks:
            near = [ext[step][b + 1]] + [ext[step][cols[k, b]] for k in range(nnb)]
            prod = dot(tiles[b], jnp.concatenate(near, axis=0))
            updates.append((load[b] - combine(prod)).astype(BF16))
        new = [lam[b] + combine(dot(prec[b], value)) for b, value in zip(blocks, updates)]
        last = step == SWEEPS - 2
        for b, value in zip(blocks, new):
            if last:
                out[b] = value.astype(BF16)
                terms = jnp.sum(value * stiff_resp[b], axis=0, keepdims=True)
                part[pl.ds(b, 1), :] = terms[:, :half] + terms[:, half:]
            else:
                lam[b] = value
                ext[step + 1][b + 1, :bs, :] = value.astype(BF16)

    def inner(work):
        @pl.loop(0, (nb - 2) // group)
        def _(g):
            work([1 + g * group + i for i in range(group)])

    first([0, nb - 1])
    halo_start(0)
    inner(first)
    for step in range(SWEEPS - 1):
        halo_wait(step)
        sweep(step, [0, nb - 1])
        if step < SWEEPS - 2:
            halo_start(step + 1)
        inner(functools.partial(sweep, step))

    def part_copy(j):
        dest = lax.rem(fr + j, n_freq)
        return pltpu.make_async_remote_copy(
            src_ref=part, dst_ref=part_recv.at[fr],
            send_sem=part_ss.at[dest], recv_sem=part_rs.at[fr],
            device_id={"freq": dest}, device_id_type=MESH,
        )

    for j in range(1, n_freq):
        part_copy(j).start()
    part_recv[fr] = part[...]
    for j in range(1, n_sub):
        idx_copy(j).wait_send()
        pack_copy(j).wait_send()
    for step in range(SWEEPS - 1):
        @pl.when(me > 0)
        def _():
            halo(step, True).wait_send()

        @pl.when(me < n_sub - 1)
        def _():
            halo(step, False).wait_send()
    for j in range(1, n_freq):
        source = lax.rem(fr + n_freq - j, n_freq)
        pltpu.make_async_remote_copy(
            src_ref=part, dst_ref=part_recv.at[source],
            send_sem=part_ss.at[source], recv_sem=part_rs.at[source],
            device_id={"freq": source}, device_id_type=MESH,
        ).wait_recv()
    total = part_recv[0]
    for p in range(1, n_freq):
        total = total + part_recv[p]
    sums = jnp.sum(total, axis=1, keepdims=True) * (1.0 / math.sqrt(bs * width))
    mine = iota(total.shape, 0) == iota(total.shape, 1)
    line = jnp.sum(jnp.where(mine, sums, 0.0), axis=0, keepdims=True)
    grad[...] = line[:, :nb]
    for j in range(1, n_freq):
        part_copy(j).wait_send()


def shards(
    n_sub, n_freq,
    response, measured, sensor_owner, sensor_row, adj_diag, adj_off, block_cols, precond, stiff_deriv,
):
    _, nb, bs, width = response.shape
    nnb = adj_off.shape[2]
    chans = measured.shape[1]
    cap = min(CAPS.get(n_sub, chans), chans)
    slots = round_up(cap, 8)
    lanes = round_up(n_sub * slots, LANES)
    halves = SWEEPS - 1
    group = next(g for g in (5, 4, 3, 2, 1) if (nb - 2) % g == 0)
    dma = pltpu.SemaphoreType.DMA
    vmem = pl.BlockSpec(memory_space=pltpu.VMEM)
    hbm = pl.BlockSpec(memory_space=pl.ANY)
    adjoint, gradient = pl.pallas_call(
        functools.partial(kernel, n_sub, n_freq, slots, group),
        out_shape=(
            jax.ShapeDtypeStruct((nb, bs, width), BF16),
            jax.ShapeDtypeStruct((1, nb), F32),
        ),
        in_specs=[hbm, vmem, vmem, vmem, hbm, hbm, pl.BlockSpec(memory_space=pltpu.SMEM), hbm, hbm],
        out_specs=(vmem, vmem),
        scratch_shapes=[
            pltpu.VMEM((nb, bs, width), BF16),
            pltpu.VMEM((nb, 2 * bs, bs), BF16),
            pltpu.VMEM((nb, nnb, 2 * bs, bs), BF16),
            pltpu.VMEM((nb, 2 * bs, bs), BF16),
            pltpu.VMEM((nb, bs, bs), BF16),
            pltpu.VMEM((nb, 2 * bs, (nnb + 1) * LANES), BF16),
            pltpu.VMEM((nb + 2, LANES, width), BF16),
            pltpu.VMEM((nb + 2, LANES, width), BF16),
            pltpu.VMEM((nb, bs, width), F32),
            pltpu.VMEM((nb, bs, width), F32),
            pltpu.VMEM((nb, bs, width), F32),
            pltpu.VMEM((nb, bs, lanes), BF16),
            pltpu.VMEM((n_sub, 1, lanes), F32),
            pltpu.VMEM((n_sub, 1, lanes), F32),
            pltpu.VMEM((n_sub, 2 * slots, width // 2), BF16),
            pltpu.VMEM((n_sub, 2 * slots, width // 2), BF16),
            pltpu.VMEM((lanes, width), F32),
            pltpu.VMEM((round_up(nb, 8), width // 2), F32),
            pltpu.VMEM((n_freq, round_up(nb, 8), width // 2), F32),
            dma((5,)),
            dma((n_sub,)), dma((n_sub,)),
            dma((n_sub,)), dma((n_sub,)),
            dma((halves, 2)), dma((halves, 2)),
            dma((n_freq,)), dma((n_freq,)),
        ],
        compiler_params=pltpu.CompilerParams(
            collective_id=0, has_side_effects=True, vmem_limit_bytes=48 * 1024 * 1024
        ),
        name="adjoint_sweeps",
    )(
        response.reshape(nb, bs, width),
        measured.reshape(chans, width),
        sensor_owner.reshape(1, chans),
        sensor_row.reshape(1, chans),
        adj_diag.reshape(nb, 2 * bs, bs),
        adj_off.reshape(nb, nnb, 2 * bs, bs),
        block_cols.T,
        precond.reshape(nb, 2 * bs, bs),
        stiff_deriv,
    )
    return adjoint[None], gradient.reshape(nb)


def solution(mesh):
    in_specs = (
        P("freq", "sub", None, None),
        P("freq", "sub", None),
        P("sub"),
        P("sub"),
        P("freq", "sub", None, None, None),
        P("freq", "sub", None, None, None, None),
        P("sub", None),
        P("freq", "sub", None, None, None),
        P("sub", None, None),
    )
    out_specs = (P("freq", "sub", None, None), P("sub"))
    body = functools.partial(shards, mesh.shape["sub"], mesh.shape["freq"])
    return jax.shard_map(body, mesh=mesh, in_specs=in_specs, out_specs=out_specs, check_vma=False)
```

```python
import functools
import math

import jax
import jax.numpy as jnp
from jax import lax
from jax.experimental import pallas as pl
from jax.experimental.pallas import tpu as pltpu
from jax.sharding import PartitionSpec as P

MESH = pl.DeviceIdType.MESH
F32 = jnp.float32
BF16 = jnp.bfloat16
SWEEPS = 3
LANES = 128
CAPS = {8: 36, 128: 3}


def round_up(value, unit):
    return -(-value // unit) * unit


def iota(shape, dim):
    return lax.broadcasted_iota(jnp.int32, shape, dim)


def one_hot(mask):
    return jnp.where(mask, 1.0, 0.0).astype(BF16)


def dot(a, b):
    return jnp.dot(a, b, preferred_element_type=F32)


def combine(prod):
    rows, half = prod.shape[0] // 2, prod.shape[1] // 2
    left = prod[:rows, :half] - prod[rows:, half:]
    right = prod[:rows, half:] + prod[rows:, :half]
    return jnp.concatenate([left, right], axis=1)


def kernel(
    n_sub, n_freq, slots, group,
    resp_hbm, meas_hbm, owner_hbm, row_hbm, diag_hbm, off_hbm, cols_hbm, prec_hbm, stiff_hbm,
    out_hbm, grad,
    out, meas, owner, row, cols, resp, diag, off, prec, stiff, tiles, ext_0, ext_1, load, lam, stiff_resp, scat,
    idx_send, idx_recv, pack_send, pack_recv, meas_all, part, part_recv,
    in_sem, out_sem, idx_ss, idx_rs, pack_ss, pack_rs, halo_ss, halo_rs, part_ss, part_rs,
):
    nb, bs, width = resp.shape
    nnb = off.shape[1]
    half = width // 2
    ext = (ext_0, ext_1)
    chans = meas.shape[0]
    lanes = scat.shape[2]
    me = lax.axis_index("sub")
    fr = lax.axis_index("freq")

    loads = [
        pltpu.make_async_copy(src, dst, in_sem.at[i])
        for i, (src, dst) in enumerate(
            [
                (owner_hbm, owner), (row_hbm, row), (meas_hbm, meas), (resp_hbm, resp), (stiff_hbm, stiff),
                (diag_hbm, diag), (off_hbm, off), (prec_hbm, prec), (cols_hbm, cols),
            ]
        )
    ]
    for copy in loads:
        copy.start()

    barrier = pltpu.get_barrier_semaphore()
    for j in range(1, n_sub):
        pl.semaphore_signal(barrier, inc=1, device_id={"sub": lax.rem(me + j, n_sub)}, device_id_type=MESH)
    for j in range(1, n_freq):
        pl.semaphore_signal(barrier, inc=1, device_id={"freq": lax.rem(fr + j, n_freq)}, device_id_type=MESH)

    loads[0].wait()
    loads[1].wait()
    own = owner[...].astype(F32)
    ri, ci = iota((chans, chans), 0), iota((chans, chans), 1)
    own_b = jnp.broadcast_to(own, (chans, chans))
    own_col = jnp.sum(jnp.where(ri == ci, own_b, 0.0), axis=1, keepdims=True)
    same = jnp.where(own_col == own_b, 1.0, 0.0)
    rank = jnp.sum(jnp.where(ri < ci, same, 0.0), axis=0, keepdims=True)
    rank_col = jnp.sum(jnp.where(ci < ri, same, 0.0), axis=1, keepdims=True)
    number = row[...].astype(F32) + 1.0
    high = jnp.floor(number * (1.0 / 64.0))
    low = number - 64.0 * high
    named = iota((n_sub, chans), 0).astype(F32) == own
    digits = jnp.concatenate([jnp.where(named, high, 0.0), jnp.where(named, low, 0.0)], axis=0).astype(BF16)
    shifted = rank_col + (me * slots).astype(F32)
    place = one_hot(iota((chans, lanes), 1).astype(F32) == shifted)
    numbers = dot(digits, place)
    numbers = numbers[:n_sub] * 64.0 + numbers[n_sub:]
    for d in range(n_sub):
        idx_send[d] = numbers[d : d + 1]
    slot = own * float(slots) + rank
    select = one_hot(iota((n_sub * slots, chans), 0).astype(F32) == slot)
    loads[2].wait()
    packed = dot(select, meas[...])
    for d in range(n_sub):
        rows = packed[d * slots : (d + 1) * slots]
        pack_send[d] = jnp.concatenate([rows[:, :half], rows[:, half:]], axis=0).astype(BF16)

    pl.semaphore_wait(barrier, n_sub - 1 + n_freq - 1)

    def idx_copy(j):
        dest = lax.rem(me + j, n_sub)
        return pltpu.make_async_remote_copy(
            src_ref=idx_send.at[dest], dst_ref=idx_recv.at[me],
            send_sem=idx_ss.at[dest], recv_sem=idx_rs.at[me],
            device_id={"sub": dest}, device_id_type=MESH,
        )

    def pack_copy(j):
        dest = lax.rem(me + j, n_sub)
        return pltpu.make_async_remote_copy(
            src_ref=pack_send.at[dest], dst_ref=pack_recv.at[me],
            send_sem=pack_ss.at[dest], recv_sem=pack_rs.at[me],
            device_id={"sub": dest}, device_id_type=MESH,
        )

    far_first = sorted(range(1, n_sub), key=lambda j: abs(j - n_sub // 2))
    for j in far_first:
        idx_copy(j).start()
    for j in far_first:
        pack_copy(j).start()
    idx_recv[me] = idx_send[me]
    pack_recv[me] = pack_send[me]

    pad = ext_0.shape[1] - bs
    for buf in ext:
        buf[:, bs:, :] = jnp.zeros((nb + 2, pad, width), BF16)
    used = n_sub * slots
    if lanes > used:
        meas_all[used:, :] = jnp.zeros((lanes - used, width), F32)
    part[...] = jnp.zeros(part.shape, F32)

    @pl.when(me == 0)
    def _():
        for buf in ext:
            buf[0, :bs, :] = jnp.zeros((bs, width), BF16)

    @pl.when(me == n_sub - 1)
    def _():
        for buf in ext:
            buf[nb + 1, :bs, :] = jnp.zeros((bs, width), BF16)

    loads[3].wait()
    loads[4].wait()

    @pl.loop(0, nb // 4)
    def _(g):
        for i in range(4):
            b = g * 4 + i
            stiff_resp[b] = dot(stiff[b], resp[b])

    loads[5].wait()
    loads[6].wait()
    for k in range(nnb + 1):
        tiles[:, :, k * LANES + bs : (k + 1) * LANES] = jnp.zeros((nb, 2 * bs, LANES - bs), BF16)

    @pl.loop(0, nb)
    def _(b):
        tiles[b, :, :bs] = diag[b]
        for k in range(nnb):
            tiles[b, :, (k + 1) * LANES : (k + 1) * LANES + bs] = off[b, k]

    for j in range(1, n_sub):
        source = lax.rem(me + n_sub - j, n_sub)
        pltpu.make_async_remote_copy(
            src_ref=idx_send.at[source], dst_ref=idx_recv.at[source],
            send_sem=idx_ss.at[source], recv_sem=idx_rs.at[source],
            device_id={"sub": source}, device_id_type=MESH,
        ).wait_recv()
    numbers = idx_recv[0]
    for p in range(1, n_sub):
        numbers = numbers + idx_recv[p]
    numbers = jnp.broadcast_to(numbers - 1.0, (bs, lanes))

    @pl.loop(0, nb // 2)
    def _(g):
        for i in range(2):
            b = g * 2 + i
            here = iota((bs, lanes), 0).astype(F32) + (b * bs).astype(F32)
            hit = jnp.where(numbers == here, 1.0, 0.0)
            scat[b] = hit.astype(BF16)
            load[b] = jnp.sum(hit, axis=1, keepdims=True) * resp[b].astype(F32)

    loads[7].wait()
    loads[8].wait()
    for j in range(1, n_sub):
        source = lax.rem(me + n_sub - j, n_sub)
        pltpu.make_async_remote_copy(
            src_ref=pack_send.at[source], dst_ref=pack_recv.at[source],
            send_sem=pack_ss.at[source], recv_sem=pack_rs.at[source],
            device_id={"sub": source}, device_id_type=MESH,
        ).wait_recv()
    for p in range(n_sub):
        rows = pack_recv[p].astype(F32)
        meas_all[p * slots : (p + 1) * slots, :] = jnp.concatenate([rows[:slots], rows[slots:]], axis=1)
    rows_in = meas_all[...].astype(BF16)

    def halo(step, low):
        src = ext[step].at[1 if low else nb, pl.ds(0, bs)]
        dst = ext[step].at[nb + 1 if low else 0, pl.ds(0, bs)]
        target = lax.rem(me + (n_sub - 1 if low else 1), n_sub)
        way = 0 if low else 1
        return pltpu.make_async_remote_copy(
            src_ref=src, dst_ref=dst, send_sem=halo_ss.at[step, way], recv_sem=halo_rs.at[step, way],
            device_id={"sub": target}, device_id_type=MESH,
        )

    def halo_start(step):
        @pl.when(me > 0)
        def _():
            halo(step, True).start()

        @pl.when(me < n_sub - 1)
        def _():
            halo(step, False).start()

    def halo_wait(step):
        @pl.when(me > 0)
        def _():
            halo(step, False).wait_recv()

        @pl.when(me < n_sub - 1)
        def _():
            halo(step, True).wait_recv()

    def first(blocks):
        rhs = [load[b] - dot(scat[b], rows_in) for b in blocks]
        for b, value in zip(blocks, rhs):
            load[b] = value
        new = [combine(dot(prec[b], value.astype(BF16))) for b, value in zip(blocks, rhs)]
        for b, value in zip(blocks, new):
            lam[b] = value
            ext_0[b + 1, :bs, :] = value.astype(BF16)

    def out_copy(b):
        return pltpu.make_async_copy(out.at[b], out_hbm.at[b], out_sem.at[b])

    def sweep(step, blocks):
        updates = []
        for b in blocks:
            near = [ext[step][b + 1]] + [ext[step][cols[k, b]] for k in range(nnb)]
            prod = dot(tiles[b], jnp.concatenate(near, axis=0))
            updates.append((load[b] - combine(prod)).astype(BF16))
        new = [lam[b] + combine(dot(prec[b], value)) for b, value in zip(blocks, updates)]
        last = step == SWEEPS - 2
        for b, value in zip(blocks, new):
            if last:
                out[b] = value.astype(BF16)
                out_copy(b).start()
                terms = jnp.sum(value * stiff_resp[b], axis=0, keepdims=True)
                part[pl.ds(b, 1), :] = terms[:, :half] + terms[:, half:]
            else:
                lam[b] = value
                ext[step + 1][b + 1, :bs, :] = value.astype(BF16)

    def inner(work):
        @pl.loop(0, (nb - 2) // group)
        def _(g):
            work([1 + g * group + i for i in range(group)])

    first([0, nb - 1])
    halo_start(0)
    inner(first)
    for step in range(SWEEPS - 1):
        halo_wait(step)
        if step < SWEEPS - 2:
            sweep(step, [0, nb - 1])
            halo_start(step + 1)
            inner(functools.partial(sweep, step))
        else:
            @pl.loop(0, nb // 4)
            def _(g):
                sweep(step, [g * 4 + i for i in range(4)])

    def part_copy(j):
        dest = lax.rem(fr + j, n_freq)
        return pltpu.make_async_remote_copy(
            src_ref=part, dst_ref=part_recv.at[fr],
            send_sem=part_ss.at[dest], recv_sem=part_rs.at[fr],
            device_id={"freq": dest}, device_id_type=MESH,
        )

    for j in range(1, n_freq):
        part_copy(j).start()
    part_recv[fr] = part[...]
    for j in range(1, n_sub):
        idx_copy(j).wait_send()
        pack_copy(j).wait_send()
    for step in range(SWEEPS - 1):
        @pl.when(me > 0)
        def _():
            halo(step, True).wait_send()

        @pl.when(me < n_sub - 1)
        def _():
            halo(step, False).wait_send()
    for j in range(1, n_freq):
        source = lax.rem(fr + n_freq - j, n_freq)
        pltpu.make_async_remote_copy(
            src_ref=part, dst_ref=part_recv.at[source],
            send_sem=part_ss.at[source], recv_sem=part_rs.at[source],
            device_id={"freq": source}, device_id_type=MESH,
        ).wait_recv()
    total = part_recv[0]
    for p in range(1, n_freq):
        total = total + part_recv[p]
    sums = jnp.sum(total, axis=1, keepdims=True) * (1.0 / math.sqrt(bs * width))
    mine = iota(total.shape, 0) == iota(total.shape, 1)
    line = jnp.sum(jnp.where(mine, sums, 0.0), axis=0, keepdims=True)
    grad[...] = line[:, :nb]
    for b in range(nb):
        out_copy(b).wait()
    for j in range(1, n_freq):
        part_copy(j).wait_send()


def shards(
    n_sub, n_freq,
    response, measured, sensor_owner, sensor_row, adj_diag, adj_off, block_cols, precond, stiff_deriv,
):
    _, nb, bs, width = response.shape
    nnb = adj_off.shape[2]
    chans = measured.shape[1]
    cap = min(CAPS.get(n_sub, chans), chans)
    slots = round_up(cap, 8)
    lanes = round_up(n_sub * slots, LANES)
    halves = SWEEPS - 1
    group = next(g for g in (5, 4, 3, 2, 1) if (nb - 2) % g == 0)
    dma = pltpu.SemaphoreType.DMA
    vmem = pl.BlockSpec(memory_space=pltpu.VMEM)
    hbm = pl.BlockSpec(memory_space=pltpu.HBM)
    adjoint, gradient = pl.pallas_call(
        functools.partial(kernel, n_sub, n_freq, slots, group),
        out_shape=(
            jax.ShapeDtypeStruct((nb, bs, width), BF16),
            jax.ShapeDtypeStruct((1, nb), F32),
        ),
        in_specs=[hbm] * 9,
        out_specs=(hbm, vmem),
        scratch_shapes=[
            pltpu.VMEM((nb, bs, width), BF16),
            pltpu.VMEM((chans, width), BF16),
            pltpu.VMEM((1, chans), jnp.int32),
            pltpu.VMEM((1, chans), jnp.int32),
            pltpu.SMEM((nnb, nb), jnp.int32),
            pltpu.VMEM((nb, bs, width), BF16),
            pltpu.VMEM((nb, 2 * bs, bs), BF16),
            pltpu.VMEM((nb, nnb, 2 * bs, bs), BF16),
            pltpu.VMEM((nb, 2 * bs, bs), BF16),
            pltpu.VMEM((nb, bs, bs), BF16),
            pltpu.VMEM((nb, 2 * bs, (nnb + 1) * LANES), BF16),
            pltpu.VMEM((nb + 2, LANES, width), BF16),
            pltpu.VMEM((nb + 2, LANES, width), BF16),
            pltpu.VMEM((nb, bs, width), F32),
            pltpu.VMEM((nb, bs, width), F32),
            pltpu.VMEM((nb, bs, width), F32),
            pltpu.VMEM((nb, bs, lanes), BF16),
            pltpu.VMEM((n_sub, 1, lanes), F32),
            pltpu.VMEM((n_sub, 1, lanes), F32),
            pltpu.VMEM((n_sub, 2 * slots, width // 2), BF16),
            pltpu.VMEM((n_sub, 2 * slots, width // 2), BF16),
            pltpu.VMEM((lanes, width), F32),
            pltpu.VMEM((round_up(nb, 8), width // 2), F32),
            pltpu.VMEM((n_freq, round_up(nb, 8), width // 2), F32),
            dma((9,)), dma((nb,)),
            dma((n_sub,)), dma((n_sub,)),
            dma((n_sub,)), dma((n_sub,)),
            dma((halves, 2)), dma((halves, 2)),
            dma((n_freq,)), dma((n_freq,)),
        ],
        compiler_params=pltpu.CompilerParams(
            collective_id=0, has_side_effects=True, vmem_limit_bytes=60 * 1024 * 1024
        ),
        name="adjoint_sweeps",
    )(
        response.reshape(nb, bs, width),
        measured.reshape(chans, width),
        sensor_owner.reshape(1, chans),
        sensor_row.reshape(1, chans),
        adj_diag.reshape(nb, 2 * bs, bs),
        adj_off.reshape(nb, nnb, 2 * bs, bs),
        block_cols.T,
        precond.reshape(nb, 2 * bs, bs),
        stiff_deriv,
    )
    return adjoint[None], gradient.reshape(nb)


def solution(mesh):
    in_specs = (
        P("freq", "sub", None, None),
        P("freq", "sub", None),
        P("sub"),
        P("sub"),
        P("freq", "sub", None, None, None),
        P("freq", "sub", None, None, None, None),
        P("sub", None),
        P("freq", "sub", None, None, None),
        P("sub", None, None),
    )
    out_specs = (P("freq", "sub", None, None), P("sub"))
    body = functools.partial(shards, mesh.shape["sub"], mesh.shape["freq"])
    return jax.shard_map(body, mesh=mesh, in_specs=in_specs, out_specs=out_specs, check_vma=False)
```

```python
import functools
import math

import jax
import jax.numpy as jnp
from jax import lax
from jax.experimental import pallas as pl
from jax.experimental.pallas import tpu as pltpu
from jax.sharding import PartitionSpec as P

MESH = pl.DeviceIdType.MESH
F32 = jnp.float32
BF16 = jnp.bfloat16
SWEEPS = 3
LANES = 128
CAPS = {8: 36, 128: 3}


def round_up(value, unit):
    return -(-value // unit) * unit


def iota(shape, dim):
    return lax.broadcasted_iota(jnp.int32, shape, dim)


def one_hot(mask):
    return jnp.where(mask, 1.0, 0.0).astype(BF16)


def dot(a, b):
    return jnp.dot(a, b, preferred_element_type=F32)


def combine(prod):
    rows, half = prod.shape[0] // 2, prod.shape[1] // 2
    left = prod[:rows, :half] - prod[rows:, half:]
    right = prod[:rows, half:] + prod[rows:, :half]
    return jnp.concatenate([left, right], axis=1)


def kernel(
    n_sub, n_freq, slots, group,
    resp_hbm, meas_hbm, owner_hbm, row_hbm, diag_hbm, off_hbm, cols_hbm, prec_hbm, stiff_hbm,
    out, grad,
    meas, owner, row, cols, resp, diag, off, prec, stiff, tiles, edge_tiles, ext_0, ext_1, hal_0, hal_1, load, rest, lam, stiff_resp, scat,
    idx_send, idx_recv, pack_send, pack_recv, meas_all, part, part_recv,
    in_sem, idx_ss, idx_rs, pack_ss, pack_rs, halo_ss, halo_rs, part_ss, part_rs,
):
    nb, bs, width = resp.shape
    nnb = off.shape[1]
    half = width // 2
    ext, hal = (ext_0, ext_1), (hal_0, hal_1)
    chans = meas.shape[0]
    lanes = scat.shape[2]
    me = lax.axis_index("sub")
    fr = lax.axis_index("freq")

    loads = [
        pltpu.make_async_copy(src, dst, in_sem.at[i])
        for i, (src, dst) in enumerate(
            [
                (owner_hbm, owner), (row_hbm, row), (meas_hbm, meas), (resp_hbm, resp), (stiff_hbm, stiff),
                (diag_hbm, diag), (off_hbm, off), (prec_hbm, prec), (cols_hbm, cols),
            ]
        )
    ]
    for copy in loads:
        copy.start()

    barrier = pltpu.get_barrier_semaphore()
    for j in range(1, n_sub):
        pl.semaphore_signal(barrier, inc=1, device_id={"sub": lax.rem(me + j, n_sub)}, device_id_type=MESH)
    for j in range(1, n_freq):
        pl.semaphore_signal(barrier, inc=1, device_id={"freq": lax.rem(fr + j, n_freq)}, device_id_type=MESH)

    pad = LANES - bs
    for buf in ext:
        buf[:, bs:, :] = jnp.zeros((nb + 2, pad, width), BF16)
        for end in (0, nb + 1):
            buf[end, :bs, :] = jnp.zeros((bs, width), BF16)
    for buf in hal:
        buf[:, bs:, :] = jnp.zeros((2, pad, width), BF16)
    for k in range(nnb + 1):
        tiles[:, :, k * LANES + bs : (k + 1) * LANES] = jnp.zeros((nb, 2 * bs, pad), BF16)
    for k in range(2):
        edge_tiles[:, :, k * LANES + bs : (k + 1) * LANES] = jnp.zeros((nb, 2 * bs, pad), BF16)
    used = n_sub * slots
    if lanes > used:
        meas_all[used:, :] = jnp.zeros((lanes - used, width), F32)
    part[...] = jnp.zeros(part.shape, F32)

    @pl.when(me == 0)
    def _():
        for buf in hal:
            buf[0, :bs, :] = jnp.zeros((bs, width), BF16)

    @pl.when(me == n_sub - 1)
    def _():
        for buf in hal:
            buf[1, :bs, :] = jnp.zeros((bs, width), BF16)

    loads[0].wait()
    loads[1].wait()
    own = owner[...].astype(F32)
    ri, ci = iota((chans, chans), 0), iota((chans, chans), 1)
    own_b = jnp.broadcast_to(own, (chans, chans))
    own_col = jnp.sum(jnp.where(ri == ci, own_b, 0.0), axis=1, keepdims=True)
    same = jnp.where(own_col == own_b, 1.0, 0.0)
    rank = jnp.sum(jnp.where(ri < ci, same, 0.0), axis=0, keepdims=True)
    rank_col = jnp.sum(jnp.where(ci < ri, same, 0.0), axis=1, keepdims=True)
    number = row[...].astype(F32) + 1.0
    high = jnp.floor(number * (1.0 / 64.0))
    low = number - 64.0 * high
    named = iota((n_sub, chans), 0).astype(F32) == own
    digits = jnp.concatenate([jnp.where(named, high, 0.0), jnp.where(named, low, 0.0)], axis=0).astype(BF16)
    shifted = rank_col + (me * slots).astype(F32)
    place = one_hot(iota((chans, lanes), 1).astype(F32) == shifted)
    numbers = dot(digits, place)
    numbers = numbers[:n_sub] * 64.0 + numbers[n_sub:]
    for d in range(n_sub):
        idx_send[d] = numbers[d : d + 1]
    slot = own * float(slots) + rank
    select = one_hot(iota((n_sub * slots, chans), 0).astype(F32) == slot)
    loads[2].wait()
    packed = dot(select, meas[...])
    for d in range(n_sub):
        rows = packed[d * slots : (d + 1) * slots]
        pack_send[d] = jnp.concatenate([rows[:, :half], rows[:, half:]], axis=0).astype(BF16)

    pl.semaphore_wait(barrier, n_sub - 1 + n_freq - 1)

    def idx_copy(j):
        dest = lax.rem(me + j, n_sub)
        return pltpu.make_async_remote_copy(
            src_ref=idx_send.at[dest], dst_ref=idx_recv.at[me],
            send_sem=idx_ss.at[dest], recv_sem=idx_rs.at[me],
            device_id={"sub": dest}, device_id_type=MESH,
        )

    def pack_copy(j):
        dest = lax.rem(me + j, n_sub)
        return pltpu.make_async_remote_copy(
            src_ref=pack_send.at[dest], dst_ref=pack_recv.at[me],
            send_sem=pack_ss.at[dest], recv_sem=pack_rs.at[me],
            device_id={"sub": dest}, device_id_type=MESH,
        )

    far_first = sorted(range(1, n_sub), key=lambda j: abs(j - n_sub // 2))
    for j in far_first:
        idx_copy(j).start()
    for j in far_first:
        pack_copy(j).start()
    idx_recv[me] = idx_send[me]
    pack_recv[me] = pack_send[me]

    loads[3].wait()
    loads[4].wait()

    @pl.loop(0, nb // 4)
    def _(g):
        for i in range(4):
            b = g * 4 + i
            stiff_resp[b] = dot(stiff[b], resp[b])

    loads[5].wait()
    loads[6].wait()
    loads[8].wait()

    @pl.loop(0, nb)
    def _(b):
        tiles[b, :, :bs] = diag[b]
        for k in range(nnb):
            tiles[b, :, (k + 1) * LANES : (k + 1) * LANES + bs] = off[b, k]
        for side, column in enumerate((0, nb + 1)):
            total = jnp.zeros((2 * bs, bs), F32)
            for k in range(nnb):
                total = total + jnp.where(cols[k, b] == column, 1.0, 0.0) * off[b, k].astype(F32)
            edge_tiles[b, :, side * LANES : side * LANES + bs] = total.astype(BF16)

    for j in range(1, n_sub):
        source = lax.rem(me + n_sub - j, n_sub)
        pltpu.make_async_remote_copy(
            src_ref=idx_send.at[source], dst_ref=idx_recv.at[source],
            send_sem=idx_ss.at[source], recv_sem=idx_rs.at[source],
            device_id={"sub": source}, device_id_type=MESH,
        ).wait_recv()
    numbers = idx_recv[0]
    for p in range(1, n_sub):
        numbers = numbers + idx_recv[p]
    numbers = jnp.broadcast_to(numbers - 1.0, (bs, lanes))

    @pl.loop(0, nb // 2)
    def _(g):
        for i in range(2):
            b = g * 2 + i
            here = iota((bs, lanes), 0).astype(F32) + (b * bs).astype(F32)
            hit = jnp.where(numbers == here, 1.0, 0.0)
            scat[b] = hit.astype(BF16)
            load[b] = jnp.sum(hit, axis=1, keepdims=True) * resp[b].astype(F32)

    loads[7].wait()
    for j in range(1, n_sub):
        source = lax.rem(me + n_sub - j, n_sub)
        pltpu.make_async_remote_copy(
            src_ref=pack_send.at[source], dst_ref=pack_recv.at[source],
            send_sem=pack_ss.at[source], recv_sem=pack_rs.at[source],
            device_id={"sub": source}, device_id_type=MESH,
        ).wait_recv()
    for p in range(n_sub):
        rows = pack_recv[p].astype(F32)
        meas_all[p * slots : (p + 1) * slots, :] = jnp.concatenate([rows[:slots], rows[slots:]], axis=1)
    rows_in = meas_all[...].astype(BF16)

    def halo(step, low):
        src = ext[step].at[1 if low else nb, pl.ds(0, bs)]
        dst = hal[step].at[1 if low else 0, pl.ds(0, bs)]
        target = lax.rem(me + (n_sub - 1 if low else 1), n_sub)
        way = 0 if low else 1
        return pltpu.make_async_remote_copy(
            src_ref=src, dst_ref=dst, send_sem=halo_ss.at[step, way], recv_sem=halo_rs.at[step, way],
            device_id={"sub": target}, device_id_type=MESH,
        )

    def halo_start(step):
        @pl.when(me > 0)
        def _():
            halo(step, True).start()

        @pl.when(me < n_sub - 1)
        def _():
            halo(step, False).start()

    def halo_wait(step):
        @pl.when(me > 0)
        def _():
            halo(step, False).wait_recv()

        @pl.when(me < n_sub - 1)
        def _():
            halo(step, True).wait_recv()

    def first(blocks):
        rhs = [load[b] - dot(scat[b], rows_in) for b in blocks]
        for b, value in zip(blocks, rhs):
            load[b] = value
        new = [combine(dot(prec[b], value.astype(BF16))) for b, value in zip(blocks, rhs)]
        for b, value in zip(blocks, new):
            lam[b] = value
            ext_0[b + 1, :bs, :] = value.astype(BF16)

    def interior(step, blocks):
        values = []
        for b in blocks:
            near = [ext[step][b + 1]] + [ext[step][cols[k, b]] for k in range(nnb)]
            values.append(load[b] - combine(dot(tiles[b], jnp.concatenate(near, axis=0))))
        for b, value in zip(blocks, values):
            rest[b] = value

    def finish(step, blocks):
        beside = hal[step][...].reshape(2 * LANES, width)
        updates = [(rest[b] - combine(dot(edge_tiles[b], beside))).astype(BF16) for b in blocks]
        new = [lam[b] + combine(dot(prec[b], value)) for b, value in zip(blocks, updates)]
        last = step == SWEEPS - 2
        for b, value in zip(blocks, new):
            if last:
                out[b] = value.astype(BF16)
                terms = jnp.sum(value * stiff_resp[b], axis=0, keepdims=True)
                part[pl.ds(b, 1), :] = terms[:, :half] + terms[:, half:]
            else:
                lam[b] = value
                ext[step + 1][b + 1, :bs, :] = value.astype(BF16)

    def inner(work):
        @pl.loop(0, (nb - 2) // group)
        def _(g):
            work([1 + g * group + i for i in range(group)])

    def every(work):
        @pl.loop(0, nb // 4)
        def _(g):
            work([g * 4 + i for i in range(4)])

    first([0, nb - 1])
    halo_start(0)
    inner(first)
    for step in range(SWEEPS - 1):
        every(functools.partial(interior, step))
        halo_wait(step)
        if step < SWEEPS - 2:
            finish(step, [0, nb - 1])
            halo_start(step + 1)
            inner(functools.partial(finish, step))
        else:
            every(functools.partial(finish, step))

    def part_copy(j):
        dest = lax.rem(fr + j, n_freq)
        return pltpu.make_async_remote_copy(
            src_ref=part, dst_ref=part_recv.at[fr],
            send_sem=part_ss.at[dest], recv_sem=part_rs.at[fr],
            device_id={"freq": dest}, device_id_type=MESH,
        )

    for j in range(1, n_freq):
        part_copy(j).start()
    part_recv[fr] = part[...]
    for j in range(1, n_sub):
        idx_copy(j).wait_send()
        pack_copy(j).wait_send()
    for step in range(SWEEPS - 1):
        @pl.when(me > 0)
        def _():
            halo(step, True).wait_send()

        @pl.when(me < n_sub - 1)
        def _():
            halo(step, False).wait_send()
    for j in range(1, n_freq):
        source = lax.rem(fr + n_freq - j, n_freq)
        pltpu.make_async_remote_copy(
            src_ref=part, dst_ref=part_recv.at[source],
            send_sem=part_ss.at[source], recv_sem=part_rs.at[source],
            device_id={"freq": source}, device_id_type=MESH,
        ).wait_recv()
    total = part_recv[0]
    for p in range(1, n_freq):
        total = total + part_recv[p]
    sums = jnp.sum(total, axis=1, keepdims=True) * (1.0 / math.sqrt(bs * width))
    mine = iota(total.shape, 0) == iota(total.shape, 1)
    line = jnp.sum(jnp.where(mine, sums, 0.0), axis=0, keepdims=True)
    grad[...] = line[:, :nb]
    for j in range(1, n_freq):
        part_copy(j).wait_send()


def shards(
    n_sub, n_freq,
    response, measured, sensor_owner, sensor_row, adj_diag, adj_off, block_cols, precond, stiff_deriv,
):
    _, nb, bs, width = response.shape
    nnb = adj_off.shape[2]
    chans = measured.shape[1]
    cap = min(CAPS.get(n_sub, chans), chans)
    slots = round_up(cap, 8)
    lanes = round_up(n_sub * slots, LANES)
    halves = SWEEPS - 1
    group = next(g for g in (5, 4, 3, 2, 1) if (nb - 2) % g == 0)
    dma = pltpu.SemaphoreType.DMA
    vmem = pl.BlockSpec(memory_space=pltpu.VMEM)
    hbm = pl.BlockSpec(memory_space=pltpu.HBM)
    adjoint, gradient = pl.pallas_call(
        functools.partial(kernel, n_sub, n_freq, slots, group),
        out_shape=(
            jax.ShapeDtypeStruct((nb, bs, width), BF16),
            jax.ShapeDtypeStruct((1, nb), F32),
        ),
        in_specs=[hbm] * 9,
        out_specs=(vmem, vmem),
        scratch_shapes=[
            pltpu.VMEM((chans, width), BF16),
            pltpu.VMEM((1, chans), jnp.int32),
            pltpu.VMEM((1, chans), jnp.int32),
            pltpu.SMEM((nnb, nb), jnp.int32),
            pltpu.VMEM((nb, bs, width), BF16),
            pltpu.VMEM((nb, 2 * bs, bs), BF16),
            pltpu.VMEM((nb, nnb, 2 * bs, bs), BF16),
            pltpu.VMEM((nb, 2 * bs, bs), BF16),
            pltpu.VMEM((nb, bs, bs), BF16),
            pltpu.VMEM((nb, 2 * bs, (nnb + 1) * LANES), BF16),
            pltpu.VMEM((nb, 2 * bs, 2 * LANES), BF16),
            pltpu.VMEM((nb + 2, LANES, width), BF16),
            pltpu.VMEM((nb + 2, LANES, width), BF16),
            pltpu.VMEM((2, LANES, width), BF16),
            pltpu.VMEM((2, LANES, width), BF16),
            pltpu.VMEM((nb, bs, width), F32),
            pltpu.VMEM((nb, bs, width), F32),
            pltpu.VMEM((nb, bs, width), F32),
            pltpu.VMEM((nb, bs, width), F32),
            pltpu.VMEM((nb, bs, lanes), BF16),
            pltpu.VMEM((n_sub, 1, lanes), F32),
            pltpu.VMEM((n_sub, 1, lanes), F32),
            pltpu.VMEM((n_sub, 2 * slots, width // 2), BF16),
            pltpu.VMEM((n_sub, 2 * slots, width // 2), BF16),
            pltpu.VMEM((lanes, width), F32),
            pltpu.VMEM((round_up(nb, 8), width // 2), F32),
            pltpu.VMEM((n_freq, round_up(nb, 8), width // 2), F32),
            dma((9,)),
            dma((n_sub,)), dma((n_sub,)),
            dma((n_sub,)), dma((n_sub,)),
            dma((halves, 2)), dma((halves, 2)),
            dma((n_freq,)), dma((n_freq,)),
        ],
        compiler_params=pltpu.CompilerParams(
            collective_id=0, has_side_effects=True, vmem_limit_bytes=48 * 1024 * 1024
        ),
        name="adjoint_sweeps",
    )(*(pltpu.with_memory_space_constraint(x, pltpu.HBM) for x in (
        response.reshape(nb, bs, width),
        measured.reshape(chans, width),
        sensor_owner.reshape(1, chans),
        sensor_row.reshape(1, chans),
        adj_diag.reshape(nb, 2 * bs, bs),
        adj_off.reshape(nb, nnb, 2 * bs, bs),
        block_cols.T,
        precond.reshape(nb, 2 * bs, bs),
        stiff_deriv,
    )))
    return adjoint[None], gradient.reshape(nb)


def solution(mesh):
    in_specs = (
        P("freq", "sub", None, None),
        P("freq", "sub", None),
        P("sub"),
        P("sub"),
        P("freq", "sub", None, None, None),
        P("freq", "sub", None, None, None, None),
        P("sub", None),
        P("freq", "sub", None, None, None),
        P("sub", None, None),
    )
    out_specs = (P("freq", "sub", None, None), P("sub"))
    body = functools.partial(shards, mesh.shape["sub"], mesh.shape["freq"])
    return jax.shard_map(body, mesh=mesh, in_specs=in_specs, out_specs=out_specs, check_vma=False)
```

```python
import functools
import math

import jax
import jax.numpy as jnp
from jax import lax
from jax.experimental import pallas as pl
from jax.experimental.pallas import tpu as pltpu
from jax.sharding import PartitionSpec as P

MESH = pl.DeviceIdType.MESH
F32 = jnp.float32
BF16 = jnp.bfloat16
SWEEPS = 3
LANES = 128
CAPS = {8: 36, 128: 3}


def round_up(value, unit):
    return -(-value // unit) * unit


def iota(shape, dim):
    return lax.broadcasted_iota(jnp.int32, shape, dim)


def one_hot(mask):
    return jnp.where(mask, 1.0, 0.0).astype(BF16)


def dot(a, b):
    return jnp.dot(a, b, preferred_element_type=F32)


def combine(prod):
    rows, half = prod.shape[0] // 2, prod.shape[1] // 2
    left = prod[:rows, :half] - prod[rows:, half:]
    right = prod[:rows, half:] + prod[rows:, :half]
    return jnp.concatenate([left, right], axis=1)


def kernel(
    n_sub, n_freq, slots, group,
    resp_hbm, meas_hbm, owner_hbm, row_hbm, diag_hbm, off_hbm, cols_hbm, prec_hbm, stiff_hbm,
    out, grad,
    meas, owner, row, cols, resp, diag, off, prec, stiff, tiles, edge_tiles, ext_0, ext_1, hal_0, hal_1, load, rest, lam, stiff_resp, scat,
    idx_send, idx_recv, pack_send, pack_recv, meas_all, part, part_recv,
    in_sem, idx_ss, idx_rs, pack_ss, pack_rs, halo_ss, halo_rs, part_ss, part_rs,
):
    nb, bs, width = resp.shape
    nnb = off.shape[1]
    half = width // 2
    ext, hal = (ext_0, ext_1), (hal_0, hal_1)
    chans = meas.shape[0]
    lanes = scat.shape[2]
    me = lax.axis_index("sub")
    fr = lax.axis_index("freq")

    loads = [
        pltpu.make_async_copy(src, dst, in_sem.at[i])
        for i, (src, dst) in enumerate(
            [
                (owner_hbm, owner), (row_hbm, row), (meas_hbm, meas), (resp_hbm, resp), (stiff_hbm, stiff),
                (diag_hbm, diag), (off_hbm, off), (prec_hbm, prec), (cols_hbm, cols),
            ]
        )
    ]
    for copy in loads:
        copy.start()

    barrier = pltpu.get_barrier_semaphore()
    for j in range(1, n_sub):
        pl.semaphore_signal(barrier, inc=1, device_id={"sub": lax.rem(me + j, n_sub)}, device_id_type=MESH)
    for j in range(1, n_freq):
        pl.semaphore_signal(barrier, inc=1, device_id={"freq": lax.rem(fr + j, n_freq)}, device_id_type=MESH)

    pad = LANES - bs
    for buf in ext:
        buf[:, bs:, :] = jnp.zeros((nb + 2, pad, width), BF16)
        for end in (0, nb + 1):
            buf[end, :bs, :] = jnp.zeros((bs, width), BF16)
    for buf in hal:
        buf[:, bs:, :] = jnp.zeros((2, pad, width), BF16)
    for k in range(nnb + 1):
        tiles[:, :, k * LANES + bs : (k + 1) * LANES] = jnp.zeros((nb, 2 * bs, pad), BF16)
    for k in range(2):
        edge_tiles[:, :, k * LANES + bs : (k + 1) * LANES] = jnp.zeros((nb, 2 * bs, pad), BF16)
    used = n_sub * slots
    if lanes > used:
        meas_all[used:, :] = jnp.zeros((lanes - used, width), F32)
    part[...] = jnp.zeros(part.shape, F32)

    @pl.when(me == 0)
    def _():
        for buf in hal:
            buf[0, :bs, :] = jnp.zeros((bs, width), BF16)

    @pl.when(me == n_sub - 1)
    def _():
        for buf in hal:
            buf[1, :bs, :] = jnp.zeros((bs, width), BF16)

    loads[0].wait()
    loads[1].wait()
    own = owner[...].astype(F32)
    ri, ci = iota((chans, chans), 0), iota((chans, chans), 1)
    own_b = jnp.broadcast_to(own, (chans, chans))
    own_col = jnp.sum(jnp.where(ri == ci, own_b, 0.0), axis=1, keepdims=True)
    same = jnp.where(own_col == own_b, 1.0, 0.0)
    rank = jnp.sum(jnp.where(ri < ci, same, 0.0), axis=0, keepdims=True)
    rank_col = jnp.sum(jnp.where(ci < ri, same, 0.0), axis=1, keepdims=True)
    number = row[...].astype(F32) + 1.0
    high = jnp.floor(number * (1.0 / 64.0))
    low = number - 64.0 * high
    named = iota((n_sub, chans), 0).astype(F32) == own
    digits = jnp.concatenate([jnp.where(named, high, 0.0), jnp.where(named, low, 0.0)], axis=0).astype(BF16)
    shifted = rank_col + (me * slots).astype(F32)
    place = one_hot(iota((chans, lanes), 1).astype(F32) == shifted)
    numbers = dot(digits, place)
    numbers = numbers[:n_sub] * 64.0 + numbers[n_sub:]
    for d in range(n_sub):
        idx_send[d] = numbers[d : d + 1]
    slot = own * float(slots) + rank
    select = one_hot(iota((n_sub * slots, chans), 0).astype(F32) == slot)
    loads[2].wait()
    packed = dot(select, meas[...])
    for d in range(n_sub):
        rows = packed[d * slots : (d + 1) * slots]
        pack_send[d] = jnp.concatenate([rows[:, :half], rows[:, half:]], axis=0).astype(BF16)

    pl.semaphore_wait(barrier, n_sub - 1 + n_freq - 1)

    def idx_copy(j):
        dest = lax.rem(me + j, n_sub)
        return pltpu.make_async_remote_copy(
            src_ref=idx_send.at[dest], dst_ref=idx_recv.at[me],
            send_sem=idx_ss.at[dest], recv_sem=idx_rs.at[me],
            device_id={"sub": dest}, device_id_type=MESH,
        )

    def pack_copy(j):
        dest = lax.rem(me + j, n_sub)
        return pltpu.make_async_remote_copy(
            src_ref=pack_send.at[dest], dst_ref=pack_recv.at[me],
            send_sem=pack_ss.at[dest], recv_sem=pack_rs.at[me],
            device_id={"sub": dest}, device_id_type=MESH,
        )

    far_first = sorted(range(1, n_sub), key=lambda j: abs(j - n_sub // 2))
    for j in far_first:
        idx_copy(j).start()
    for j in far_first:
        pack_copy(j).start()
    idx_recv[me] = idx_send[me]
    pack_recv[me] = pack_send[me]

    for i in (3, 4, 5, 6, 8):
        loads[i].wait()

    @pl.loop(0, nb // 2)
    def _(g):
        for b in (g * 2, g * 2 + 1):
            stiff_resp[b] = dot(stiff[b], resp[b])
            tiles[b, :, :bs] = diag[b]
            for k in range(nnb):
                tiles[b, :, (k + 1) * LANES : (k + 1) * LANES + bs] = off[b, k]
            for side, column in enumerate((0, nb + 1)):
                total = jnp.zeros((2 * bs, bs), BF16)
                for k in range(nnb):
                    reads = jnp.full((2 * bs, bs), jnp.where(cols[k, b] == column, 1.0, 0.0), F32).astype(BF16)
                    total = total + reads * off[b, k]
                edge_tiles[b, :, side * LANES : side * LANES + bs] = total

    for j in range(1, n_sub):
        source = lax.rem(me + n_sub - j, n_sub)
        pltpu.make_async_remote_copy(
            src_ref=idx_send.at[source], dst_ref=idx_recv.at[source],
            send_sem=idx_ss.at[source], recv_sem=idx_rs.at[source],
            device_id={"sub": source}, device_id_type=MESH,
        ).wait_recv()
    numbers = idx_recv[0]
    for p in range(1, n_sub):
        numbers = numbers + idx_recv[p]
    numbers = jnp.broadcast_to(numbers - 1.0, (bs, lanes))

    @pl.loop(0, nb // 4)
    def _(g):
        for i in range(4):
            b = g * 4 + i
            here = iota((bs, lanes), 0).astype(F32) + (b * bs).astype(F32)
            hit = jnp.where(numbers == here, 1.0, 0.0)
            scat[b] = hit.astype(BF16)
            load[b] = jnp.sum(hit, axis=1, keepdims=True) * resp[b].astype(F32)

    loads[7].wait()
    for j in range(1, n_sub):
        source = lax.rem(me + n_sub - j, n_sub)
        pltpu.make_async_remote_copy(
            src_ref=pack_send.at[source], dst_ref=pack_recv.at[source],
            send_sem=pack_ss.at[source], recv_sem=pack_rs.at[source],
            device_id={"sub": source}, device_id_type=MESH,
        ).wait_recv()
    for p in range(n_sub):
        rows = pack_recv[p].astype(F32)
        meas_all[p * slots : (p + 1) * slots, :] = jnp.concatenate([rows[:slots], rows[slots:]], axis=1)
    rows_in = meas_all[...].astype(BF16)

    def halo(step, low):
        src = ext[step].at[1 if low else nb, pl.ds(0, bs)]
        dst = hal[step].at[1 if low else 0, pl.ds(0, bs)]
        target = lax.rem(me + (n_sub - 1 if low else 1), n_sub)
        way = 0 if low else 1
        return pltpu.make_async_remote_copy(
            src_ref=src, dst_ref=dst, send_sem=halo_ss.at[step, way], recv_sem=halo_rs.at[step, way],
            device_id={"sub": target}, device_id_type=MESH,
        )

    def halo_start(step):
        @pl.when(me > 0)
        def _():
            halo(step, True).start()

        @pl.when(me < n_sub - 1)
        def _():
            halo(step, False).start()

    def halo_wait(step):
        @pl.when(me > 0)
        def _():
            halo(step, False).wait_recv()

        @pl.when(me < n_sub - 1)
        def _():
            halo(step, True).wait_recv()

    def first(blocks):
        rhs = [load[b] - dot(scat[b], rows_in) for b in blocks]
        for b, value in zip(blocks, rhs):
            load[b] = value
        new = [combine(dot(prec[b], value.astype(BF16))) for b, value in zip(blocks, rhs)]
        for b, value in zip(blocks, new):
            lam[b] = value
            ext_0[b + 1, :bs, :] = value.astype(BF16)

    def interior(step, blocks):
        values = []
        for b in blocks:
            near = [ext[step][b + 1]] + [ext[step][cols[k, b]] for k in range(nnb)]
            values.append(load[b] - combine(dot(tiles[b], jnp.concatenate(near, axis=0))))
        for b, value in zip(blocks, values):
            rest[b] = value

    def finish(step, blocks):
        beside = hal[step][...].reshape(2 * LANES, width)
        updates = [(rest[b] - combine(dot(edge_tiles[b], beside))).astype(BF16) for b in blocks]
        new = [lam[b] + combine(dot(prec[b], value)) for b, value in zip(blocks, updates)]
        last = step == SWEEPS - 2
        for b, value in zip(blocks, new):
            if last:
                out[b] = value.astype(BF16)
                terms = jnp.sum(value * stiff_resp[b], axis=0, keepdims=True)
                part[pl.ds(b, 1), :] = terms[:, :half] + terms[:, half:]
            else:
                lam[b] = value
                ext[step + 1][b + 1, :bs, :] = value.astype(BF16)

    def inner(work):
        for g in range(0, nb - 2, group):
            work([1 + g + i for i in range(group)])

    def every(work):
        for g in range(0, nb, 4):
            work([g + i for i in range(4)])

    first([0, nb - 1])
    halo_start(0)
    inner(first)
    for step in range(SWEEPS - 1):
        every(functools.partial(interior, step))
        halo_wait(step)
        if step < SWEEPS - 2:
            finish(step, [0, nb - 1])
            halo_start(step + 1)
            inner(functools.partial(finish, step))
        else:
            every(functools.partial(finish, step))

    def part_copy(j):
        dest = lax.rem(fr + j, n_freq)
        return pltpu.make_async_remote_copy(
            src_ref=part, dst_ref=part_recv.at[fr],
            send_sem=part_ss.at[dest], recv_sem=part_rs.at[fr],
            device_id={"freq": dest}, device_id_type=MESH,
        )

    for j in range(1, n_freq):
        part_copy(j).start()
    part_recv[fr] = part[...]
    for j in range(1, n_sub):
        idx_copy(j).wait_send()
        pack_copy(j).wait_send()
    for step in range(SWEEPS - 1):
        @pl.when(me > 0)
        def _():
            halo(step, True).wait_send()

        @pl.when(me < n_sub - 1)
        def _():
            halo(step, False).wait_send()
    for j in range(1, n_freq):
        source = lax.rem(fr + n_freq - j, n_freq)
        pltpu.make_async_remote_copy(
            src_ref=part, dst_ref=part_recv.at[source],
            send_sem=part_ss.at[source], recv_sem=part_rs.at[source],
            device_id={"freq": source}, device_id_type=MESH,
        ).wait_recv()
    total = part_recv[0]
    for p in range(1, n_freq):
        total = total + part_recv[p]
    sums = jnp.sum(total, axis=1, keepdims=True) * (1.0 / math.sqrt(bs * width))
    mine = iota(total.shape, 0) == iota(total.shape, 1)
    line = jnp.sum(jnp.where(mine, sums, 0.0), axis=0, keepdims=True)
    grad[...] = line[:, :nb]
    for j in range(1, n_freq):
        part_copy(j).wait_send()


def shards(
    n_sub, n_freq,
    response, measured, sensor_owner, sensor_row, adj_diag, adj_off, block_cols, precond, stiff_deriv,
):
    _, nb, bs, width = response.shape
    nnb = adj_off.shape[2]
    chans = measured.shape[1]
    cap = min(CAPS.get(n_sub, chans), chans)
    slots = round_up(cap, 8)
    lanes = round_up(n_sub * slots, LANES)
    halves = SWEEPS - 1
    group = next(g for g in (5, 4, 3, 2, 1) if (nb - 2) % g == 0)
    dma = pltpu.SemaphoreType.DMA
    vmem = pl.BlockSpec(memory_space=pltpu.VMEM)
    hbm = pl.BlockSpec(memory_space=pltpu.HBM)
    adjoint, gradient = pl.pallas_call(
        functools.partial(kernel, n_sub, n_freq, slots, group),
        out_shape=(
            jax.ShapeDtypeStruct((nb, bs, width), BF16),
            jax.ShapeDtypeStruct((1, nb), F32),
        ),
        in_specs=[hbm] * 9,
        out_specs=(vmem, vmem),
        scratch_shapes=[
            pltpu.VMEM((chans, width), BF16),
            pltpu.VMEM((1, chans), jnp.int32),
            pltpu.VMEM((1, chans), jnp.int32),
            pltpu.SMEM((nnb, nb), jnp.int32),
            pltpu.VMEM((nb, bs, width), BF16),
            pltpu.VMEM((nb, 2 * bs, bs), BF16),
            pltpu.VMEM((nb, nnb, 2 * bs, bs), BF16),
            pltpu.VMEM((nb, 2 * bs, bs), BF16),
            pltpu.VMEM((nb, bs, bs), BF16),
            pltpu.VMEM((nb, 2 * bs, (nnb + 1) * LANES), BF16),
            pltpu.VMEM((nb, 2 * bs, 2 * LANES), BF16),
            pltpu.VMEM((nb + 2, LANES, width), BF16),
            pltpu.VMEM((nb + 2, LANES, width), BF16),
            pltpu.VMEM((2, LANES, width), BF16),
            pltpu.VMEM((2, LANES, width), BF16),
            pltpu.VMEM((nb, bs, width), F32),
            pltpu.VMEM((nb, bs, width), F32),
            pltpu.VMEM((nb, bs, width), F32),
            pltpu.VMEM((nb, bs, width), F32),
            pltpu.VMEM((nb, bs, lanes), BF16),
            pltpu.VMEM((n_sub, 1, lanes), F32),
            pltpu.VMEM((n_sub, 1, lanes), F32),
            pltpu.VMEM((n_sub, 2 * slots, width // 2), BF16),
            pltpu.VMEM((n_sub, 2 * slots, width // 2), BF16),
            pltpu.VMEM((lanes, width), F32),
            pltpu.VMEM((round_up(nb, 8), width // 2), F32),
            pltpu.VMEM((n_freq, round_up(nb, 8), width // 2), F32),
            dma((9,)),
            dma((n_sub,)), dma((n_sub,)),
            dma((n_sub,)), dma((n_sub,)),
            dma((halves, 2)), dma((halves, 2)),
            dma((n_freq,)), dma((n_freq,)),
        ],
        compiler_params=pltpu.CompilerParams(
            collective_id=0, has_side_effects=True, vmem_limit_bytes=48 * 1024 * 1024
        ),
        name="adjoint_sweeps",
    )(*(pltpu.with_memory_space_constraint(x, pltpu.HBM) for x in (
        response.reshape(nb, bs, width),
        measured.reshape(chans, width),
        sensor_owner.reshape(1, chans),
        sensor_row.reshape(1, chans),
        adj_diag.reshape(nb, 2 * bs, bs),
        adj_off.reshape(nb, nnb, 2 * bs, bs),
        block_cols.T,
        precond.reshape(nb, 2 * bs, bs),
        stiff_deriv,
    )))
    return adjoint[None], gradient.reshape(nb)


def solution(mesh):
    in_specs = (
        P("freq", "sub", None, None),
        P("freq", "sub", None),
        P("sub"),
        P("sub"),
        P("freq", "sub", None, None, None),
        P("freq", "sub", None, None, None, None),
        P("sub", None),
        P("freq", "sub", None, None, None),
        P("sub", None, None),
    )
    out_specs = (P("freq", "sub", None, None), P("sub"))
    body = functools.partial(shards, mesh.shape["sub"], mesh.shape["freq"])
    return jax.shard_map(body, mesh=mesh, in_specs=in_specs, out_specs=out_specs, check_vma=False)
```

```python
import functools
import math

import jax
import jax.numpy as jnp
from jax import lax
from jax.experimental import pallas as pl
from jax.experimental.pallas import tpu as pltpu
from jax.sharding import PartitionSpec as P

MESH = pl.DeviceIdType.MESH
F32 = jnp.float32
BF16 = jnp.bfloat16
SWEEPS = 3
LANES = 128
CAPS = {8: 36, 128: 3}


def round_up(value, unit):
    return -(-value // unit) * unit


def iota(shape, dim):
    return lax.broadcasted_iota(jnp.int32, shape, dim)


def one_hot(mask):
    return jnp.where(mask, 1.0, 0.0).astype(BF16)


def dot(a, b):
    return jnp.dot(a, b, preferred_element_type=F32)


def combine(prod):
    rows, half = prod.shape[0] // 2, prod.shape[1] // 2
    left = prod[:rows, :half] - prod[rows:, half:]
    right = prod[:rows, half:] + prod[rows:, :half]
    return jnp.concatenate([left, right], axis=1)


def kernel(
    n_sub, n_freq, slots, group,
    resp_hbm, meas_hbm, owner_hbm, row_hbm, diag_hbm, off_hbm, cols_hbm, prec_hbm, stiff_hbm,
    out, grad,
    meas, owner, row, cols, resp, diag, off, prec, stiff, tiles, edge_tiles, ext_0, ext_1, hal_0, hal_1, load, rest, lam, upd, stiff_resp, tee, scat,
    idx_send, idx_recv, pack_send, pack_recv, meas_all, part, part_recv,
    in_sem, idx_ss, idx_rs, pack_ss, pack_rs, halo_ss, halo_rs, part_ss, part_rs,
):
    nb, bs, width = resp.shape
    nnb = off.shape[1]
    half = width // 2
    ext, hal = (ext_0, ext_1), (hal_0, hal_1)
    chans = meas.shape[0]
    lanes = scat.shape[2]
    me = lax.axis_index("sub")
    fr = lax.axis_index("freq")

    loads = [
        pltpu.make_async_copy(src, dst, in_sem.at[i])
        for i, (src, dst) in enumerate(
            [
                (owner_hbm, owner), (row_hbm, row), (meas_hbm, meas), (resp_hbm, resp), (stiff_hbm, stiff),
                (diag_hbm, diag), (off_hbm, off), (prec_hbm, prec), (cols_hbm, cols),
            ]
        )
    ]
    for copy in loads:
        copy.start()

    barrier = pltpu.get_barrier_semaphore()
    for j in range(1, n_sub):
        pl.semaphore_signal(barrier, inc=1, device_id={"sub": lax.rem(me + j, n_sub)}, device_id_type=MESH)
    for j in range(1, n_freq):
        pl.semaphore_signal(barrier, inc=1, device_id={"freq": lax.rem(fr + j, n_freq)}, device_id_type=MESH)

    pad = LANES - bs
    for buf in ext:
        buf[:, bs:, :] = jnp.zeros((nb + 2, pad, width), BF16)
        for end in (0, nb + 1):
            buf[end, :bs, :] = jnp.zeros((bs, width), BF16)
    for buf in hal:
        buf[:, bs:, :] = jnp.zeros((2, pad, width), BF16)
    for k in range(nnb + 1):
        tiles[:, :, k * LANES + bs : (k + 1) * LANES] = jnp.zeros((nb, 2 * bs, pad), BF16)
    for k in range(2):
        edge_tiles[:, :, k * LANES + bs : (k + 1) * LANES] = jnp.zeros((nb, 2 * bs, pad), BF16)
    used = n_sub * slots
    if lanes > used:
        meas_all[used:, :] = jnp.zeros((lanes - used, width), F32)
    part[...] = jnp.zeros(part.shape, F32)

    @pl.when(me == 0)
    def _():
        for buf in hal:
            buf[0, :bs, :] = jnp.zeros((bs, width), BF16)

    @pl.when(me == n_sub - 1)
    def _():
        for buf in hal:
            buf[1, :bs, :] = jnp.zeros((bs, width), BF16)

    loads[0].wait()
    loads[1].wait()
    own = owner[...].astype(F32)
    ri, ci = iota((chans, chans), 0), iota((chans, chans), 1)
    own_b = jnp.broadcast_to(own, (chans, chans))
    own_col = jnp.sum(jnp.where(ri == ci, own_b, 0.0), axis=1, keepdims=True)
    same = jnp.where(own_col == own_b, 1.0, 0.0)
    rank = jnp.sum(jnp.where(ri < ci, same, 0.0), axis=0, keepdims=True)
    rank_col = jnp.sum(jnp.where(ci < ri, same, 0.0), axis=1, keepdims=True)
    number = row[...].astype(F32) + 1.0
    high = jnp.floor(number * (1.0 / 64.0))
    low = number - 64.0 * high
    named = iota((n_sub, chans), 0).astype(F32) == own
    digits = jnp.concatenate([jnp.where(named, high, 0.0), jnp.where(named, low, 0.0)], axis=0).astype(BF16)
    shifted = rank_col + (me * slots).astype(F32)
    place = one_hot(iota((chans, lanes), 1).astype(F32) == shifted)
    numbers = dot(digits, place)
    numbers = numbers[:n_sub] * 64.0 + numbers[n_sub:]
    for d in range(n_sub):
        idx_send[d] = numbers[d : d + 1]
    slot = own * float(slots) + rank
    select = one_hot(iota((n_sub * slots, chans), 0).astype(F32) == slot)
    loads[2].wait()
    packed = dot(select, meas[...])
    for d in range(n_sub):
        rows = packed[d * slots : (d + 1) * slots]
        pack_send[d] = jnp.concatenate([rows[:, :half], rows[:, half:]], axis=0).astype(BF16)

    pl.semaphore_wait(barrier, n_sub - 1 + n_freq - 1)

    def idx_copy(j):
        dest = lax.rem(me + j, n_sub)
        return pltpu.make_async_remote_copy(
            src_ref=idx_send.at[dest], dst_ref=idx_recv.at[me],
            send_sem=idx_ss.at[dest], recv_sem=idx_rs.at[me],
            device_id={"sub": dest}, device_id_type=MESH,
        )

    def pack_copy(j):
        dest = lax.rem(me + j, n_sub)
        return pltpu.make_async_remote_copy(
            src_ref=pack_send.at[dest], dst_ref=pack_recv.at[me],
            send_sem=pack_ss.at[dest], recv_sem=pack_rs.at[me],
            device_id={"sub": dest}, device_id_type=MESH,
        )

    far_first = sorted(range(1, n_sub), key=lambda j: abs(j - n_sub // 2))
    for j in far_first:
        idx_copy(j).start()
    for j in far_first:
        pack_copy(j).start()
    idx_recv[me] = idx_send[me]
    pack_recv[me] = pack_send[me]

    for i in (3, 4, 5, 6, 7, 8):
        loads[i].wait()

    @pl.loop(0, nb // 2)
    def _(g):
        for b in (g * 2, g * 2 + 1):
            value = dot(stiff[b], resp[b])
            stiff_resp[b] = value
            turned = jnp.concatenate([value[:, half:], -value[:, :half]], axis=1)
            tee[b] = lax.dot_general(
                prec[b], jnp.concatenate([value, turned], axis=0).astype(BF16),
                (((0,), (0,)), ((), ())), preferred_element_type=F32,
            )
            tiles[b, :, :bs] = diag[b]
            for k in range(nnb):
                tiles[b, :, (k + 1) * LANES : (k + 1) * LANES + bs] = off[b, k]
            for side, column in enumerate((0, nb + 1)):
                total = jnp.zeros((2 * bs, bs), BF16)
                for k in range(nnb):
                    reads = jnp.full((2 * bs, bs), jnp.where(cols[k, b] == column, 1.0, 0.0), F32).astype(BF16)
                    total = total + reads * off[b, k]
                edge_tiles[b, :, side * LANES : side * LANES + bs] = total

    for j in range(1, n_sub):
        source = lax.rem(me + n_sub - j, n_sub)
        pltpu.make_async_remote_copy(
            src_ref=idx_send.at[source], dst_ref=idx_recv.at[source],
            send_sem=idx_ss.at[source], recv_sem=idx_rs.at[source],
            device_id={"sub": source}, device_id_type=MESH,
        ).wait_recv()
    numbers = idx_recv[0]
    for p in range(1, n_sub):
        numbers = numbers + idx_recv[p]
    numbers = jnp.broadcast_to(numbers - 1.0, (bs, lanes))

    @pl.loop(0, nb // 4)
    def _(g):
        for i in range(4):
            b = g * 4 + i
            here = iota((bs, lanes), 0).astype(F32) + (b * bs).astype(F32)
            hit = jnp.where(numbers == here, 1.0, 0.0)
            scat[b] = hit.astype(BF16)
            load[b] = jnp.sum(hit, axis=1, keepdims=True) * resp[b].astype(F32)

    for j in range(1, n_sub):
        source = lax.rem(me + n_sub - j, n_sub)
        pltpu.make_async_remote_copy(
            src_ref=pack_send.at[source], dst_ref=pack_recv.at[source],
            send_sem=pack_ss.at[source], recv_sem=pack_rs.at[source],
            device_id={"sub": source}, device_id_type=MESH,
        ).wait_recv()
    for p in range(n_sub):
        rows = pack_recv[p].astype(F32)
        meas_all[p * slots : (p + 1) * slots, :] = jnp.concatenate([rows[:slots], rows[slots:]], axis=1)
    rows_in = meas_all[...].astype(BF16)

    def halo(step, low):
        src = ext[step].at[1 if low else nb, pl.ds(0, bs)]
        dst = hal[step].at[1 if low else 0, pl.ds(0, bs)]
        target = lax.rem(me + (n_sub - 1 if low else 1), n_sub)
        way = 0 if low else 1
        return pltpu.make_async_remote_copy(
            src_ref=src, dst_ref=dst, send_sem=halo_ss.at[step, way], recv_sem=halo_rs.at[step, way],
            device_id={"sub": target}, device_id_type=MESH,
        )

    def halo_start(step):
        @pl.when(me > 0)
        def _():
            halo(step, True).start()

        @pl.when(me < n_sub - 1)
        def _():
            halo(step, False).start()

    def halo_wait(step):
        @pl.when(me > 0)
        def _():
            halo(step, False).wait_recv()

        @pl.when(me < n_sub - 1)
        def _():
            halo(step, True).wait_recv()

    def first(blocks):
        rhs = [load[b] - dot(scat[b], rows_in) for b in blocks]
        for b, value in zip(blocks, rhs):
            load[b] = value
        new = [combine(dot(prec[b], value.astype(BF16))) for b, value in zip(blocks, rhs)]
        for b, value in zip(blocks, new):
            lam[b] = value
            ext_0[b + 1, :bs, :] = value.astype(BF16)

    def interior(step, blocks):
        values = []
        for b in blocks:
            near = [ext[step][b + 1]] + [ext[step][cols[k, b]] for k in range(nnb)]
            values.append(load[b] - combine(dot(tiles[b], jnp.concatenate(near, axis=0))))
        for b, value in zip(blocks, values):
            rest[b] = value
            if step == SWEEPS - 2:
                terms = jnp.sum(lam[b] * stiff_resp[b], axis=0, keepdims=True)
                part[b : b + 1, :] = terms[:, :half] + terms[:, half:]

    def updates(step, blocks):
        beside = hal[step][...].reshape(2 * LANES, width)
        return [(rest[b] - combine(dot(edge_tiles[b], beside))).astype(BF16) for b in blocks]

    def finish(step, blocks):
        values = updates(step, blocks)
        new = [lam[b] + combine(dot(prec[b], value)) for b, value in zip(blocks, values)]
        for b, value in zip(blocks, new):
            lam[b] = value
            ext[step + 1][b + 1, :bs, :] = value.astype(BF16)

    def last_updates(blocks):
        for b, value in zip(blocks, updates(SWEEPS - 2, blocks)):
            upd[b] = value
            terms = jnp.sum(value.astype(F32) * tee[b], axis=0, keepdims=True)
            part[b : b + 1, :] += terms[:, :half] + terms[:, half:]

    def last_products(blocks):
        for b in blocks:
            out[b] = (lam[b] + combine(dot(prec[b], upd[b]))).astype(BF16)

    def inner(work):
        for g in range(0, nb - 2, group):
            work([1 + g + i for i in range(group)])

    def every(work):
        for g in range(0, nb, 4):
            work([g + i for i in range(4)])

    first([0, nb - 1])
    halo_start(0)
    inner(first)
    for step in range(SWEEPS - 1):
        every(functools.partial(interior, step))
        halo_wait(step)
        if step < SWEEPS - 2:
            finish(step, [0, nb - 1])
            halo_start(step + 1)
            inner(functools.partial(finish, step))
        else:
            every(last_updates)

    def part_copy(j):
        dest = lax.rem(fr + j, n_freq)
        return pltpu.make_async_remote_copy(
            src_ref=part, dst_ref=part_recv.at[fr],
            send_sem=part_ss.at[dest], recv_sem=part_rs.at[fr],
            device_id={"freq": dest}, device_id_type=MESH,
        )

    for j in range(1, n_freq):
        part_copy(j).start()
    part_recv[fr] = part[...]
    every(last_products)
    for j in range(1, n_sub):
        idx_copy(j).wait_send()
        pack_copy(j).wait_send()
    for step in range(SWEEPS - 1):
        @pl.when(me > 0)
        def _():
            halo(step, True).wait_send()

        @pl.when(me < n_sub - 1)
        def _():
            halo(step, False).wait_send()
    for j in range(1, n_freq):
        source = lax.rem(fr + n_freq - j, n_freq)
        pltpu.make_async_remote_copy(
            src_ref=part, dst_ref=part_recv.at[source],
            send_sem=part_ss.at[source], recv_sem=part_rs.at[source],
            device_id={"freq": source}, device_id_type=MESH,
        ).wait_recv()
    total = part_recv[0]
    for p in range(1, n_freq):
        total = total + part_recv[p]
    sums = jnp.sum(total, axis=1, keepdims=True) * (1.0 / math.sqrt(bs * width))
    mine = iota(total.shape, 0) == iota(total.shape, 1)
    line = jnp.sum(jnp.where(mine, sums, 0.0), axis=0, keepdims=True)
    grad[...] = line[:, :nb]
    for j in range(1, n_freq):
        part_copy(j).wait_send()


def close(adjoint_in, gradient_in, adjoint, gradient, sems):
    copies = [
        pltpu.make_async_copy(adjoint_in, adjoint, sems.at[0]),
        pltpu.make_async_copy(gradient_in, gradient, sems.at[1]),
    ]
    for copy in copies:
        copy.start()
    for copy in copies:
        copy.wait()


def shards(
    n_sub, n_freq,
    response, measured, sensor_owner, sensor_row, adj_diag, adj_off, block_cols, precond, stiff_deriv,
):
    _, nb, bs, width = response.shape
    nnb = adj_off.shape[2]
    chans = measured.shape[1]
    cap = min(CAPS.get(n_sub, chans), chans)
    slots = round_up(cap, 8)
    lanes = round_up(n_sub * slots, LANES)
    halves = SWEEPS - 1
    group = next(g for g in (5, 4, 3, 2, 1) if (nb - 2) % g == 0)
    dma = pltpu.SemaphoreType.DMA
    vmem = pl.BlockSpec(memory_space=pltpu.VMEM)
    hbm = pl.BlockSpec(memory_space=pltpu.HBM)
    adjoint, gradient = pl.pallas_call(
        functools.partial(kernel, n_sub, n_freq, slots, group),
        out_shape=(
            jax.ShapeDtypeStruct((nb, bs, width), BF16),
            jax.ShapeDtypeStruct((1, nb), F32),
        ),
        in_specs=[hbm] * 9,
        out_specs=(vmem, vmem),
        scratch_shapes=[
            pltpu.VMEM((chans, width), BF16),
            pltpu.VMEM((1, chans), jnp.int32),
            pltpu.VMEM((1, chans), jnp.int32),
            pltpu.SMEM((nnb, nb), jnp.int32),
            pltpu.VMEM((nb, bs, width), BF16),
            pltpu.VMEM((nb, 2 * bs, bs), BF16),
            pltpu.VMEM((nb, nnb, 2 * bs, bs), BF16),
            pltpu.VMEM((nb, 2 * bs, bs), BF16),
            pltpu.VMEM((nb, bs, bs), BF16),
            pltpu.VMEM((nb, 2 * bs, (nnb + 1) * LANES), BF16),
            pltpu.VMEM((nb, 2 * bs, 2 * LANES), BF16),
            pltpu.VMEM((nb + 2, LANES, width), BF16),
            pltpu.VMEM((nb + 2, LANES, width), BF16),
            pltpu.VMEM((2, LANES, width), BF16),
            pltpu.VMEM((2, LANES, width), BF16),
            pltpu.VMEM((nb, bs, width), F32),
            pltpu.VMEM((nb, bs, width), F32),
            pltpu.VMEM((nb, bs, width), F32),
            pltpu.VMEM((nb, bs, width), BF16),
            pltpu.VMEM((nb, bs, width), F32),
            pltpu.VMEM((nb, bs, width), F32),
            pltpu.VMEM((nb, bs, lanes), BF16),
            pltpu.VMEM((n_sub, 1, lanes), F32),
            pltpu.VMEM((n_sub, 1, lanes), F32),
            pltpu.VMEM((n_sub, 2 * slots, width // 2), BF16),
            pltpu.VMEM((n_sub, 2 * slots, width // 2), BF16),
            pltpu.VMEM((lanes, width), F32),
            pltpu.VMEM((round_up(nb, 8), width // 2), F32),
            pltpu.VMEM((n_freq, round_up(nb, 8), width // 2), F32),
            dma((9,)),
            dma((n_sub,)), dma((n_sub,)),
            dma((n_sub,)), dma((n_sub,)),
            dma((halves, 2)), dma((halves, 2)),
            dma((n_freq,)), dma((n_freq,)),
        ],
        compiler_params=pltpu.CompilerParams(
            collective_id=0, has_side_effects=True, vmem_limit_bytes=48 * 1024 * 1024
        ),
        name="adjoint_sweeps",
    )(*(pltpu.with_memory_space_constraint(x, pltpu.HBM) for x in (
        response.reshape(nb, bs, width),
        measured.reshape(chans, width),
        sensor_owner.reshape(1, chans),
        sensor_row.reshape(1, chans),
        adj_diag.reshape(nb, 2 * bs, bs),
        adj_off.reshape(nb, nnb, 2 * bs, bs),
        block_cols.T,
        precond.reshape(nb, 2 * bs, bs),
        stiff_deriv,
    )))
    adjoint, gradient = pl.pallas_call(
        close,
        out_shape=(
            jax.ShapeDtypeStruct((nb, bs, width), BF16),
            jax.ShapeDtypeStruct((1, nb), F32),
        ),
        in_specs=[pl.BlockSpec(memory_space=pl.ANY)] * 2,
        out_specs=(hbm, hbm),
        scratch_shapes=[dma((2,))],
        name="results",
    )(adjoint, gradient)
    return adjoint[None], gradient.reshape(nb)


def solution(mesh):
    in_specs = (
        P("freq", "sub", None, None),
        P("freq", "sub", None),
        P("sub"),
        P("sub"),
        P("freq", "sub", None, None, None),
        P("freq", "sub", None, None, None, None),
        P("sub", None),
        P("freq", "sub", None, None, None),
        P("sub", None, None),
    )
    out_specs = (P("freq", "sub", None, None), P("sub"))
    body = functools.partial(shards, mesh.shape["sub"], mesh.shape["freq"])
    return jax.shard_map(body, mesh=mesh, in_specs=in_specs, out_specs=out_specs, check_vma=False)
```

```python
import functools
import math

import jax
import jax.numpy as jnp
from jax import lax
from jax.experimental import pallas as pl
from jax.experimental.pallas import tpu as pltpu
from jax.sharding import PartitionSpec as P

MESH = pl.DeviceIdType.MESH
F32 = jnp.float32
BF16 = jnp.bfloat16
SWEEPS = 3
LANES = 128
CAPS = {8: 36, 128: 3}


def round_up(value, unit):
    return -(-value // unit) * unit


def iota(shape, dim):
    return lax.broadcasted_iota(jnp.int32, shape, dim)


def one_hot(mask):
    return jnp.where(mask, 1.0, 0.0).astype(BF16)


def dot(a, b):
    return jnp.dot(a, b, preferred_element_type=F32)


def combine(prod):
    rows, half = prod.shape[0] // 2, prod.shape[1] // 2
    left = prod[:rows, :half] - prod[rows:, half:]
    right = prod[:rows, half:] + prod[rows:, :half]
    return jnp.concatenate([left, right], axis=1)


def kernel(
    n_sub, n_freq, slots, group,
    resp_hbm, meas_hbm, owner_hbm, row_hbm, diag_hbm, off_hbm, cols_hbm, prec_hbm, stiff_hbm,
    out, grad,
    meas, owner, row, cols, resp, diag, off, prec, stiff, tiles, edge_tiles, ext_0, ext_1, hal_0, hal_1, load, rest, lam, upd, stiff_resp, tee, scat,
    idx_send, idx_recv, pack_send, pack_recv, meas_all, part, part_recv,
    in_sem, idx_ss, idx_rs, pack_ss, pack_rs, halo_ss, halo_rs, part_ss, part_rs,
):
    nb, bs, width = resp.shape
    nnb = off.shape[1]
    half = width // 2
    ext, hal = (ext_0, ext_1), (hal_0, hal_1)
    chans = meas.shape[0]
    lanes = scat.shape[2]
    me = lax.axis_index("sub")
    fr = lax.axis_index("freq")

    loads = [
        pltpu.make_async_copy(src, dst, in_sem.at[i])
        for i, (src, dst) in enumerate(
            [
                (owner_hbm, owner), (row_hbm, row), (meas_hbm, meas), (resp_hbm, resp), (stiff_hbm, stiff),
                (diag_hbm, diag), (off_hbm, off), (prec_hbm, prec), (cols_hbm, cols),
            ]
        )
    ]
    for copy in loads:
        copy.start()

    barrier = pltpu.get_barrier_semaphore()
    for j in range(1, n_sub):
        pl.semaphore_signal(barrier, inc=1, device_id={"sub": lax.rem(me + j, n_sub)}, device_id_type=MESH)
    for j in range(1, n_freq):
        pl.semaphore_signal(barrier, inc=1, device_id={"freq": lax.rem(fr + j, n_freq)}, device_id_type=MESH)

    pad = LANES - bs
    for buf in ext:
        buf[:, bs:, :] = jnp.zeros((nb + 2, pad, width), BF16)
        for end in (0, nb + 1):
            buf[end, :bs, :] = jnp.zeros((bs, width), BF16)
    for buf in hal:
        buf[:, bs:, :] = jnp.zeros((2, pad, width), BF16)
    for k in range(nnb + 1):
        tiles[:, :, k * LANES + bs : (k + 1) * LANES] = jnp.zeros((nb, 2 * bs, pad), BF16)
    for k in range(2):
        edge_tiles[:, :, k * LANES + bs : (k + 1) * LANES] = jnp.zeros((nb, 2 * bs, pad), BF16)
    used = n_sub * slots
    if lanes > used:
        meas_all[used:, :] = jnp.zeros((lanes - used, width), F32)
    part[...] = jnp.zeros(part.shape, F32)

    @pl.when(me == 0)
    def _():
        for buf in hal:
            buf[0, :bs, :] = jnp.zeros((bs, width), BF16)

    @pl.when(me == n_sub - 1)
    def _():
        for buf in hal:
            buf[1, :bs, :] = jnp.zeros((bs, width), BF16)

    loads[0].wait()
    loads[1].wait()
    own = owner[...].astype(F32)
    ri, ci = iota((chans, chans), 0), iota((chans, chans), 1)
    own_b = jnp.broadcast_to(own, (chans, chans))
    own_col = jnp.sum(jnp.where(ri == ci, own_b, 0.0), axis=1, keepdims=True)
    same = jnp.where(own_col == own_b, 1.0, 0.0)
    rank = jnp.sum(jnp.where(ri < ci, same, 0.0), axis=0, keepdims=True)
    rank_col = jnp.sum(jnp.where(ci < ri, same, 0.0), axis=1, keepdims=True)
    number = row[...].astype(F32) + 1.0
    high = jnp.floor(number * (1.0 / 64.0))
    low = number - 64.0 * high
    named = iota((n_sub, chans), 0).astype(F32) == own
    digits = jnp.concatenate([jnp.where(named, high, 0.0), jnp.where(named, low, 0.0)], axis=0).astype(BF16)
    shifted = rank_col + (me * slots).astype(F32)
    place = one_hot(iota((chans, lanes), 1).astype(F32) == shifted)
    numbers = dot(digits, place)
    numbers = numbers[:n_sub] * 64.0 + numbers[n_sub:]
    for d in range(n_sub):
        idx_send[d] = numbers[d : d + 1]
    slot = own * float(slots) + rank
    select = one_hot(iota((n_sub * slots, chans), 0).astype(F32) == slot)
    loads[2].wait()
    packed = dot(select, meas[...])
    for d in range(n_sub):
        rows = packed[d * slots : (d + 1) * slots]
        pack_send[d] = jnp.concatenate([rows[:, :half], rows[:, half:]], axis=0).astype(BF16)

    pl.semaphore_wait(barrier, n_sub - 1 + n_freq - 1)

    def idx_copy(j):
        dest = lax.rem(me + j, n_sub)
        return pltpu.make_async_remote_copy(
            src_ref=idx_send.at[dest], dst_ref=idx_recv.at[me],
            send_sem=idx_ss.at[dest], recv_sem=idx_rs.at[me],
            device_id={"sub": dest}, device_id_type=MESH,
        )

    def pack_copy(j):
        dest = lax.rem(me + j, n_sub)
        return pltpu.make_async_remote_copy(
            src_ref=pack_send.at[dest], dst_ref=pack_recv.at[me],
            send_sem=pack_ss.at[dest], recv_sem=pack_rs.at[me],
            device_id={"sub": dest}, device_id_type=MESH,
        )

    far_first = sorted(range(1, n_sub), key=lambda j: abs(j - n_sub // 2))
    for j in far_first:
        idx_copy(j).start()
    for j in far_first:
        pack_copy(j).start()
    idx_recv[me] = idx_send[me]
    pack_recv[me] = pack_send[me]

    for i in (3, 4, 5, 6, 7, 8):
        loads[i].wait()

    @pl.loop(0, nb // 2)
    def _(g):
        for b in (g * 2, g * 2 + 1):
            value = dot(stiff[b], resp[b])
            stiff_resp[b] = value
            turned = jnp.concatenate([value[:, half:], -value[:, :half]], axis=1)
            tee[b] = lax.dot_general(
                prec[b], jnp.concatenate([value, turned], axis=0).astype(BF16),
                (((0,), (0,)), ((), ())), preferred_element_type=F32,
            )
            tiles[b, :, :bs] = diag[b]
            for k in range(nnb):
                tiles[b, :, (k + 1) * LANES : (k + 1) * LANES + bs] = off[b, k]
            for side, column in enumerate((0, nb + 1)):
                total = jnp.zeros((2 * bs, bs), BF16)
                for k in range(nnb):
                    reads = jnp.full((2 * bs, bs), jnp.where(cols[k, b] == column, 1.0, 0.0), F32).astype(BF16)
                    total = total + reads * off[b, k]
                edge_tiles[b, :, side * LANES : side * LANES + bs] = total

    for j in range(1, n_sub):
        source = lax.rem(me + n_sub - j, n_sub)
        pltpu.make_async_remote_copy(
            src_ref=idx_send.at[source], dst_ref=idx_recv.at[source],
            send_sem=idx_ss.at[source], recv_sem=idx_rs.at[source],
            device_id={"sub": source}, device_id_type=MESH,
        ).wait_recv()
    numbers = idx_recv[0]
    for p in range(1, n_sub):
        numbers = numbers + idx_recv[p]
    numbers = jnp.broadcast_to(numbers - 1.0, (bs, lanes))

    @pl.loop(0, nb // 4)
    def _(g):
        for i in range(4):
            b = g * 4 + i
            here = iota((bs, lanes), 0).astype(F32) + (b * bs).astype(F32)
            hit = jnp.where(numbers == here, 1.0, 0.0)
            scat[b] = hit.astype(BF16)
            load[b] = jnp.sum(hit, axis=1, keepdims=True) * resp[b].astype(F32)

    def place_rows(source):
        rows = pack_recv[source].astype(F32)
        spot = pl.multiple_of(source * slots, 8)
        meas_all[pl.ds(spot, slots), :] = jnp.concatenate([rows[:slots], rows[slots:]], axis=1)

    place_rows(me)
    for j in reversed(far_first):
        source = lax.rem(me + n_sub - j, n_sub)
        pltpu.make_async_remote_copy(
            src_ref=pack_send.at[source], dst_ref=pack_recv.at[source],
            send_sem=pack_ss.at[source], recv_sem=pack_rs.at[source],
            device_id={"sub": source}, device_id_type=MESH,
        ).wait_recv()
        place_rows(source)
    rows_in = meas_all[...].astype(BF16)

    def halo(step, low):
        src = ext[step].at[1 if low else nb, pl.ds(0, bs)]
        dst = hal[step].at[1 if low else 0, pl.ds(0, bs)]
        target = lax.rem(me + (n_sub - 1 if low else 1), n_sub)
        way = 0 if low else 1
        return pltpu.make_async_remote_copy(
            src_ref=src, dst_ref=dst, send_sem=halo_ss.at[step, way], recv_sem=halo_rs.at[step, way],
            device_id={"sub": target}, device_id_type=MESH,
        )

    def halo_start(step):
        @pl.when(me > 0)
        def _():
            halo(step, True).start()

        @pl.when(me < n_sub - 1)
        def _():
            halo(step, False).start()

    def halo_wait(step):
        @pl.when(me > 0)
        def _():
            halo(step, False).wait_recv()

        @pl.when(me < n_sub - 1)
        def _():
            halo(step, True).wait_recv()

    def first(blocks):
        rhs = [load[b] - dot(scat[b], rows_in) for b in blocks]
        for b, value in zip(blocks, rhs):
            load[b] = value
        new = [combine(dot(prec[b], value.astype(BF16))) for b, value in zip(blocks, rhs)]
        for b, value in zip(blocks, new):
            lam[b] = value
            ext_0[b + 1, :bs, :] = value.astype(BF16)

    def interior(step, blocks):
        values = []
        for b in blocks:
            near = [ext[step][b + 1]] + [ext[step][cols[k, b]] for k in range(nnb)]
            values.append(load[b] - combine(dot(tiles[b], jnp.concatenate(near, axis=0))))
        for b, value in zip(blocks, values):
            rest[b] = value
            if step == SWEEPS - 2:
                terms = jnp.sum(lam[b] * stiff_resp[b], axis=0, keepdims=True)
                part[b : b + 1, :] = terms[:, :half] + terms[:, half:]

    def updates(step, blocks):
        beside = hal[step][...].reshape(2 * LANES, width)
        return [(rest[b] - combine(dot(edge_tiles[b], beside))).astype(BF16) for b in blocks]

    def finish(step, blocks):
        values = updates(step, blocks)
        new = [lam[b] + combine(dot(prec[b], value)) for b, value in zip(blocks, values)]
        for b, value in zip(blocks, new):
            lam[b] = value
            ext[step + 1][b + 1, :bs, :] = value.astype(BF16)

    def last_updates(blocks):
        for b, value in zip(blocks, updates(SWEEPS - 2, blocks)):
            upd[b] = value
            terms = jnp.sum(value.astype(F32) * tee[b], axis=0, keepdims=True)
            part[b : b + 1, :] += terms[:, :half] + terms[:, half:]

    def last_products(blocks):
        for b in blocks:
            out[b] = (lam[b] + combine(dot(prec[b], upd[b]))).astype(BF16)

    def edges(work):
        work([0, nb - 1])
        work([1 + i for i in range(group)])

    def inner(work):
        for g in range(group, nb - 2, group):
            work([1 + g + i for i in range(group)])

    def every(work):
        for g in range(0, nb, 4):
            work([g + i for i in range(4)])

    edges(first)
    halo_start(0)
    inner(first)
    for step in range(SWEEPS - 1):
        every(functools.partial(interior, step))
        halo_wait(step)
        if step < SWEEPS - 2:
            edges(functools.partial(finish, step))
            halo_start(step + 1)
            inner(functools.partial(finish, step))
        else:
            every(last_updates)

    def part_copy(j):
        dest = lax.rem(fr + j, n_freq)
        return pltpu.make_async_remote_copy(
            src_ref=part, dst_ref=part_recv.at[fr],
            send_sem=part_ss.at[dest], recv_sem=part_rs.at[fr],
            device_id={"freq": dest}, device_id_type=MESH,
        )

    for j in range(1, n_freq):
        part_copy(j).start()
    part_recv[fr] = part[...]
    every(last_products)
    for j in range(1, n_sub):
        idx_copy(j).wait_send()
        pack_copy(j).wait_send()
    for step in range(SWEEPS - 1):
        @pl.when(me > 0)
        def _():
            halo(step, True).wait_send()

        @pl.when(me < n_sub - 1)
        def _():
            halo(step, False).wait_send()
    for j in range(1, n_freq):
        source = lax.rem(fr + n_freq - j, n_freq)
        pltpu.make_async_remote_copy(
            src_ref=part, dst_ref=part_recv.at[source],
            send_sem=part_ss.at[source], recv_sem=part_rs.at[source],
            device_id={"freq": source}, device_id_type=MESH,
        ).wait_recv()
    total = part_recv[0]
    for p in range(1, n_freq):
        total = total + part_recv[p]
    sums = jnp.sum(total, axis=1, keepdims=True) * (1.0 / math.sqrt(bs * width))
    mine = iota(total.shape, 0) == iota(total.shape, 1)
    line = jnp.sum(jnp.where(mine, sums, 0.0), axis=0, keepdims=True)
    grad[...] = line[:, :nb]
    for j in range(1, n_freq):
        part_copy(j).wait_send()


def close(adjoint_in, gradient_in, adjoint, gradient, sems):
    copies = [
        pltpu.make_async_copy(adjoint_in, adjoint, sems.at[0]),
        pltpu.make_async_copy(gradient_in, gradient, sems.at[1]),
    ]
    for copy in copies:
        copy.start()
    for copy in copies:
        copy.wait()


def shards(
    n_sub, n_freq,
    response, measured, sensor_owner, sensor_row, adj_diag, adj_off, block_cols, precond, stiff_deriv,
):
    _, nb, bs, width = response.shape
    nnb = adj_off.shape[2]
    chans = measured.shape[1]
    cap = min(CAPS.get(n_sub, chans), chans)
    slots = round_up(cap, 8)
    lanes = round_up(n_sub * slots, LANES)
    halves = SWEEPS - 1
    group = next(g for g in (5, 4, 3, 2, 1) if (nb - 2) % g == 0)
    dma = pltpu.SemaphoreType.DMA
    vmem = pl.BlockSpec(memory_space=pltpu.VMEM)
    hbm = pl.BlockSpec(memory_space=pltpu.HBM)
    adjoint, gradient = pl.pallas_call(
        functools.partial(kernel, n_sub, n_freq, slots, group),
        out_shape=(
            jax.ShapeDtypeStruct((nb, bs, width), BF16),
            jax.ShapeDtypeStruct((1, nb), F32),
        ),
        in_specs=[hbm] * 9,
        out_specs=(vmem, vmem),
        scratch_shapes=[
            pltpu.VMEM((chans, width), BF16),
            pltpu.VMEM((1, chans), jnp.int32),
            pltpu.VMEM((1, chans), jnp.int32),
            pltpu.SMEM((nnb, nb), jnp.int32),
            pltpu.VMEM((nb, bs, width), BF16),
            pltpu.VMEM((nb, 2 * bs, bs), BF16),
            pltpu.VMEM((nb, nnb, 2 * bs, bs), BF16),
            pltpu.VMEM((nb, 2 * bs, bs), BF16),
            pltpu.VMEM((nb, bs, bs), BF16),
            pltpu.VMEM((nb, 2 * bs, (nnb + 1) * LANES), BF16),
            pltpu.VMEM((nb, 2 * bs, 2 * LANES), BF16),
            pltpu.VMEM((nb + 2, LANES, width), BF16),
            pltpu.VMEM((nb + 2, LANES, width), BF16),
            pltpu.VMEM((2, LANES, width), BF16),
            pltpu.VMEM((2, LANES, width), BF16),
            pltpu.VMEM((nb, bs, width), F32),
            pltpu.VMEM((nb, bs, width), F32),
            pltpu.VMEM((nb, bs, width), F32),
            pltpu.VMEM((nb, bs, width), BF16),
            pltpu.VMEM((nb, bs, width), F32),
            pltpu.VMEM((nb, bs, width), F32),
            pltpu.VMEM((nb, bs, lanes), BF16),
            pltpu.VMEM((n_sub, 1, lanes), F32),
            pltpu.VMEM((n_sub, 1, lanes), F32),
            pltpu.VMEM((n_sub, 2 * slots, width // 2), BF16),
            pltpu.VMEM((n_sub, 2 * slots, width // 2), BF16),
            pltpu.VMEM((lanes, width), F32),
            pltpu.VMEM((round_up(nb, 8), width // 2), F32),
            pltpu.VMEM((n_freq, round_up(nb, 8), width // 2), F32),
            dma((9,)),
            dma((n_sub,)), dma((n_sub,)),
            dma((n_sub,)), dma((n_sub,)),
            dma((halves, 2)), dma((halves, 2)),
            dma((n_freq,)), dma((n_freq,)),
        ],
        compiler_params=pltpu.CompilerParams(
            collective_id=0, has_side_effects=True, vmem_limit_bytes=48 * 1024 * 1024
        ),
        name="adjoint_sweeps",
    )(*(pltpu.with_memory_space_constraint(x, pltpu.HBM) for x in (
        response.reshape(nb, bs, width),
        measured.reshape(chans, width),
        sensor_owner.reshape(1, chans),
        sensor_row.reshape(1, chans),
        adj_diag.reshape(nb, 2 * bs, bs),
        adj_off.reshape(nb, nnb, 2 * bs, bs),
        block_cols.T,
        precond.reshape(nb, 2 * bs, bs),
        stiff_deriv,
    )))
    adjoint, gradient = pl.pallas_call(
        close,
        out_shape=(
            jax.ShapeDtypeStruct((nb, bs, width), BF16),
            jax.ShapeDtypeStruct((1, nb), F32),
        ),
        in_specs=[vmem, vmem],
        out_specs=(hbm, hbm),
        scratch_shapes=[dma((2,))],
        name="results",
    )(adjoint, gradient)
    return adjoint[None], gradient.reshape(nb)


def solution(mesh):
    in_specs = (
        P("freq", "sub", None, None),
        P("freq", "sub", None),
        P("sub"),
        P("sub"),
        P("freq", "sub", None, None, None),
        P("freq", "sub", None, None, None, None),
        P("sub", None),
        P("freq", "sub", None, None, None),
        P("sub", None, None),
    )
    out_specs = (P("freq", "sub", None, None), P("sub"))
    body = functools.partial(shards, mesh.shape["sub"], mesh.shape["freq"])
    return jax.shard_map(body, mesh=mesh, in_specs=in_specs, out_specs=out_specs, check_vma=False)
```

```python
import functools
import math

import jax
import jax.numpy as jnp
from jax import lax
from jax.experimental import pallas as pl
from jax.experimental.pallas import tpu as pltpu
from jax.sharding import PartitionSpec as P

MESH = pl.DeviceIdType.MESH
F32 = jnp.float32
BF16 = jnp.bfloat16
SWEEPS = 3
LANES = 128
CAPS = {8: 36, 128: 3}


def round_up(value, unit):
    return -(-value // unit) * unit


def iota(shape, dim):
    return lax.broadcasted_iota(jnp.int32, shape, dim)


def one_hot(mask):
    return jnp.where(mask, 1.0, 0.0).astype(BF16)


def dot(a, b):
    return jnp.dot(a, b, preferred_element_type=F32)


def combine(prod):
    rows, half = prod.shape[0] // 2, prod.shape[1] // 2
    left = prod[:rows, :half] - prod[rows:, half:]
    right = prod[:rows, half:] + prod[rows:, :half]
    return jnp.concatenate([left, right], axis=1)


def kernel(
    n_sub, n_freq, slots, group,
    resp_hbm, meas_hbm, owner_hbm, row_hbm, diag_hbm, off_hbm, cols_hbm, prec_hbm, stiff_hbm,
    out, grad,
    meas, owner, row, cols, resp, diag, off, prec, stiff, tiles, edge_tiles, ext_0, ext_1, hal_0, hal_1, load, rest, lam, upd, stiff_resp, tee, scat,
    idx_send, idx_recv, pack_send, pack_recv, meas_all, part, part_recv,
    in_sem, idx_ss, idx_rs, pack_ss, pack_rs, halo_ss, halo_rs, part_ss, part_rs,
):
    nb, bs, width = resp.shape
    nnb = off.shape[1]
    half = width // 2
    ext, hal = (ext_0, ext_1), (hal_0, hal_1)
    chans = meas.shape[0]
    lanes = scat.shape[2]
    me = lax.axis_index("sub")
    fr = lax.axis_index("freq")

    loads = [
        pltpu.make_async_copy(src, dst, in_sem.at[i])
        for i, (src, dst) in enumerate(
            [
                (owner_hbm, owner), (row_hbm, row), (meas_hbm, meas), (resp_hbm, resp), (stiff_hbm, stiff),
                (diag_hbm, diag), (off_hbm, off), (prec_hbm, prec), (cols_hbm, cols),
            ]
        )
    ]
    for copy in loads:
        copy.start()

    barrier = pltpu.get_barrier_semaphore()
    for j in range(1, n_sub):
        pl.semaphore_signal(barrier, inc=1, device_id={"sub": lax.rem(me + j, n_sub)}, device_id_type=MESH)
    for j in range(1, n_freq):
        pl.semaphore_signal(barrier, inc=1, device_id={"freq": lax.rem(fr + j, n_freq)}, device_id_type=MESH)

    pad = LANES - bs
    for buf in ext:
        buf[:, bs:, :] = jnp.zeros((nb + 2, pad, width), BF16)
        for end in (0, nb + 1):
            buf[end, :bs, :] = jnp.zeros((bs, width), BF16)
    for buf in hal:
        buf[:, bs:, :] = jnp.zeros((2, pad, width), BF16)
    for k in range(nnb + 1):
        tiles[:, :, k * LANES + bs : (k + 1) * LANES] = jnp.zeros((nb, 2 * bs, pad), BF16)
    for k in range(2):
        edge_tiles[:, :, k * LANES + bs : (k + 1) * LANES] = jnp.zeros((nb, 2 * bs, pad), BF16)
    used = n_sub * slots
    if lanes > used:
        meas_all[used:, :] = jnp.zeros((lanes - used, width), F32)
    part[...] = jnp.zeros(part.shape, F32)

    @pl.when(me == 0)
    def _():
        for buf in hal:
            buf[0, :bs, :] = jnp.zeros((bs, width), BF16)

    @pl.when(me == n_sub - 1)
    def _():
        for buf in hal:
            buf[1, :bs, :] = jnp.zeros((bs, width), BF16)

    loads[0].wait()
    loads[1].wait()
    own = owner[...].astype(F32)
    ri, ci = iota((chans, chans), 0), iota((chans, chans), 1)
    own_b = jnp.broadcast_to(own, (chans, chans))
    own_col = jnp.sum(jnp.where(ri == ci, own_b, 0.0), axis=1, keepdims=True)
    same = jnp.where(own_col == own_b, 1.0, 0.0)
    rank = jnp.sum(jnp.where(ri < ci, same, 0.0), axis=0, keepdims=True)
    rank_col = jnp.sum(jnp.where(ci < ri, same, 0.0), axis=1, keepdims=True)
    number = row[...].astype(F32) + 1.0
    high = jnp.floor(number * (1.0 / 64.0))
    low = number - 64.0 * high
    named = iota((n_sub, chans), 0).astype(F32) == own
    digits = jnp.concatenate([jnp.where(named, high, 0.0), jnp.where(named, low, 0.0)], axis=0).astype(BF16)
    shifted = rank_col + (me * slots).astype(F32)
    place = one_hot(iota((chans, lanes), 1).astype(F32) == shifted)
    numbers = dot(digits, place)
    numbers = numbers[:n_sub] * 64.0 + numbers[n_sub:]
    for d in range(n_sub):
        idx_send[d] = numbers[d : d + 1]
    slot = own * float(slots) + rank
    select = one_hot(iota((n_sub * slots, chans), 0).astype(F32) == slot)
    loads[2].wait()
    packed = dot(select, meas[...])
    for d in range(n_sub):
        rows = packed[d * slots : (d + 1) * slots]
        pack_send[d] = jnp.concatenate([rows[:, :half], rows[:, half:]], axis=0).astype(BF16)

    pl.semaphore_wait(barrier, n_sub - 1 + n_freq - 1)

    def idx_copy(j):
        dest = lax.rem(me + j, n_sub)
        return pltpu.make_async_remote_copy(
            src_ref=idx_send.at[dest], dst_ref=idx_recv.at[me],
            send_sem=idx_ss.at[dest], recv_sem=idx_rs.at[me],
            device_id={"sub": dest}, device_id_type=MESH,
        )

    def pack_copy(j):
        dest = lax.rem(me + j, n_sub)
        return pltpu.make_async_remote_copy(
            src_ref=pack_send.at[dest], dst_ref=pack_recv.at[me],
            send_sem=pack_ss.at[dest], recv_sem=pack_rs.at[me],
            device_id={"sub": dest}, device_id_type=MESH,
        )

    far_first = sorted(range(1, n_sub), key=lambda j: abs(j - n_sub // 2))
    for j in far_first:
        idx_copy(j).start()
    for j in far_first:
        pack_copy(j).start()
    idx_recv[me] = idx_send[me]
    pack_recv[me] = pack_send[me]

    for i in (3, 4, 5, 6, 7, 8):
        loads[i].wait()

    @pl.loop(0, nb // 2)
    def _(g):
        for b in (g * 2, g * 2 + 1):
            value = dot(stiff[b], resp[b])
            stiff_resp[b] = value
            turned = jnp.concatenate([value[:, half:], -value[:, :half]], axis=1)
            tee[b] = lax.dot_general(
                prec[b], jnp.concatenate([value, turned], axis=0).astype(BF16),
                (((0,), (0,)), ((), ())), preferred_element_type=F32,
            )
            tiles[b, :, :bs] = diag[b]
            for k in range(nnb):
                tiles[b, :, (k + 1) * LANES : (k + 1) * LANES + bs] = off[b, k]
            for side, column in enumerate((0, nb + 1)):
                total = jnp.zeros((2 * bs, bs), BF16)
                for k in range(nnb):
                    reads = jnp.full((2 * bs, bs), jnp.where(cols[k, b] == column, 1.0, 0.0), F32).astype(BF16)
                    total = total + reads * off[b, k]
                edge_tiles[b, :, side * LANES : side * LANES + bs] = total

    for j in range(1, n_sub):
        source = lax.rem(me + n_sub - j, n_sub)
        pltpu.make_async_remote_copy(
            src_ref=idx_send.at[source], dst_ref=idx_recv.at[source],
            send_sem=idx_ss.at[source], recv_sem=idx_rs.at[source],
            device_id={"sub": source}, device_id_type=MESH,
        ).wait_recv()
    numbers = idx_recv[0]
    for p in range(1, n_sub):
        numbers = numbers + idx_recv[p]
    numbers = jnp.broadcast_to(numbers - 1.0, (bs, lanes))

    @pl.loop(0, nb // 4)
    def _(g):
        for i in range(4):
            b = g * 4 + i
            here = iota((bs, lanes), 0).astype(F32) + (b * bs).astype(F32)
            hit = jnp.where(numbers == here, 1.0, 0.0)
            scat[b] = hit.astype(BF16)
            load[b] = jnp.sum(hit, axis=1, keepdims=True) * resp[b].astype(F32)

    for j in range(1, n_sub):
        source = lax.rem(me + n_sub - j, n_sub)
        pltpu.make_async_remote_copy(
            src_ref=pack_send.at[source], dst_ref=pack_recv.at[source],
            send_sem=pack_ss.at[source], recv_sem=pack_rs.at[source],
            device_id={"sub": source}, device_id_type=MESH,
        ).wait_recv()
    for p in range(n_sub):
        rows = pack_recv[p].astype(F32)
        meas_all[p * slots : (p + 1) * slots, :] = jnp.concatenate([rows[:slots], rows[slots:]], axis=1)
    rows_in = meas_all[...].astype(BF16)

    def halo(step, low):
        src = ext[step].at[1 if low else nb, pl.ds(0, bs)]
        dst = hal[step].at[1 if low else 0, pl.ds(0, bs)]
        target = lax.rem(me + (n_sub - 1 if low else 1), n_sub)
        way = 0 if low else 1
        return pltpu.make_async_remote_copy(
            src_ref=src, dst_ref=dst, send_sem=halo_ss.at[step, way], recv_sem=halo_rs.at[step, way],
            device_id={"sub": target}, device_id_type=MESH,
        )

    def halo_start(step):
        @pl.when(me > 0)
        def _():
            halo(step, True).start()

        @pl.when(me < n_sub - 1)
        def _():
            halo(step, False).start()

    def halo_wait(step):
        @pl.when(me > 0)
        def _():
            halo(step, False).wait_recv()

        @pl.when(me < n_sub - 1)
        def _():
            halo(step, True).wait_recv()

    def first(blocks):
        rhs = [load[b] - dot(scat[b], rows_in) for b in blocks]
        for b, value in zip(blocks, rhs):
            load[b] = value
        new = [combine(dot(prec[b], value.astype(BF16))) for b, value in zip(blocks, rhs)]
        for b, value in zip(blocks, new):
            lam[b] = value
            ext_0[b + 1, :bs, :] = value.astype(BF16)

    def interior(step, blocks):
        values = []
        for b in blocks:
            near = [ext[step][b + 1]] + [ext[step][cols[k, b]] for k in range(nnb)]
            values.append(load[b] - combine(dot(tiles[b], jnp.concatenate(near, axis=0))))
        for b, value in zip(blocks, values):
            rest[b] = value
            if step == SWEEPS - 2:
                terms = jnp.sum(lam[b] * stiff_resp[b], axis=0, keepdims=True)
                part[b : b + 1, :] = terms[:, :half] + terms[:, half:]

    def updates(step, blocks):
        beside = hal[step][...].reshape(2 * LANES, width)
        return [(rest[b] - combine(dot(edge_tiles[b], beside))).astype(BF16) for b in blocks]

    def finish(step, blocks):
        values = updates(step, blocks)
        new = [lam[b] + combine(dot(prec[b], value)) for b, value in zip(blocks, values)]
        for b, value in zip(blocks, new):
            lam[b] = value
            ext[step + 1][b + 1, :bs, :] = value.astype(BF16)

    def last_updates(blocks):
        for b, value in zip(blocks, updates(SWEEPS - 2, blocks)):
            upd[b] = value
            terms = jnp.sum(value.astype(F32) * tee[b], axis=0, keepdims=True)
            part[b : b + 1, :] += terms[:, :half] + terms[:, half:]

    def last_products(blocks):
        for b in blocks:
            out[b] = (lam[b] + combine(dot(prec[b], upd[b]))).astype(BF16)

    def inner(work):
        for g in range(0, nb - 2, group):
            work([1 + g + i for i in range(group)])

    def every(work):
        for g in range(0, nb, 4):
            work([g + i for i in range(4)])

    first([0, nb - 1])
    halo_start(0)
    inner(first)
    for step in range(SWEEPS - 1):
        every(functools.partial(interior, step))
        halo_wait(step)
        if step < SWEEPS - 2:
            finish(step, [0, nb - 1])
            halo_start(step + 1)
            inner(functools.partial(finish, step))
        else:
            every(last_updates)

    def part_copy(j):
        dest = lax.rem(fr + j, n_freq)
        return pltpu.make_async_remote_copy(
            src_ref=part, dst_ref=part_recv.at[fr],
            send_sem=part_ss.at[dest], recv_sem=part_rs.at[fr],
            device_id={"freq": dest}, device_id_type=MESH,
        )

    for j in range(1, n_freq):
        part_copy(j).start()
    part_recv[fr] = part[...]
    every(last_products)
    for j in range(1, n_sub):
        idx_copy(j).wait_send()
        pack_copy(j).wait_send()
    for step in range(SWEEPS - 1):
        @pl.when(me > 0)
        def _():
            halo(step, True).wait_send()

        @pl.when(me < n_sub - 1)
        def _():
            halo(step, False).wait_send()
    for j in range(1, n_freq):
        source = lax.rem(fr + n_freq - j, n_freq)
        pltpu.make_async_remote_copy(
            src_ref=part, dst_ref=part_recv.at[source],
            send_sem=part_ss.at[source], recv_sem=part_rs.at[source],
            device_id={"freq": source}, device_id_type=MESH,
        ).wait_recv()
    total = part_recv[0]
    for p in range(1, n_freq):
        total = total + part_recv[p]
    sums = jnp.sum(total, axis=1, keepdims=True) * (1.0 / math.sqrt(bs * width))
    mine = iota(total.shape, 0) == iota(total.shape, 1)
    line = jnp.sum(jnp.where(mine, sums, 0.0), axis=0, keepdims=True)
    grad[...] = line[:, :nb]
    for j in range(1, n_freq):
        part_copy(j).wait_send()


def shards(
    n_sub, n_freq,
    response, measured, sensor_owner, sensor_row, adj_diag, adj_off, block_cols, precond, stiff_deriv,
):
    _, nb, bs, width = response.shape
    nnb = adj_off.shape[2]
    chans = measured.shape[1]
    cap = min(CAPS.get(n_sub, chans), chans)
    slots = round_up(cap, 8)
    lanes = round_up(n_sub * slots, LANES)
    halves = SWEEPS - 1
    group = next(g for g in (5, 4, 3, 2, 1) if (nb - 2) % g == 0)
    dma = pltpu.SemaphoreType.DMA
    vmem = pl.BlockSpec(memory_space=pltpu.VMEM)
    hbm = pl.BlockSpec(memory_space=pltpu.HBM)
    adjoint, gradient = pl.pallas_call(
        functools.partial(kernel, n_sub, n_freq, slots, group),
        out_shape=(
            jax.ShapeDtypeStruct((nb, bs, width), BF16),
            jax.ShapeDtypeStruct((1, nb), F32),
        ),
        in_specs=[hbm] * 9,
        out_specs=(vmem, vmem),
        scratch_shapes=[
            pltpu.VMEM((chans, width), BF16),
            pltpu.VMEM((1, chans), jnp.int32),
            pltpu.VMEM((1, chans), jnp.int32),
            pltpu.SMEM((nnb, nb), jnp.int32),
            pltpu.VMEM((nb, bs, width), BF16),
            pltpu.VMEM((nb, 2 * bs, bs), BF16),
            pltpu.VMEM((nb, nnb, 2 * bs, bs), BF16),
            pltpu.VMEM((nb, 2 * bs, bs), BF16),
            pltpu.VMEM((nb, bs, bs), BF16),
            pltpu.VMEM((nb, 2 * bs, (nnb + 1) * LANES), BF16),
            pltpu.VMEM((nb, 2 * bs, 2 * LANES), BF16),
            pltpu.VMEM((nb + 2, LANES, width), BF16),
            pltpu.VMEM((nb + 2, LANES, width), BF16),
            pltpu.VMEM((2, LANES, width), BF16),
            pltpu.VMEM((2, LANES, width), BF16),
            pltpu.VMEM((nb, bs, width), F32),
            pltpu.VMEM((nb, bs, width), F32),
            pltpu.VMEM((nb, bs, width), F32),
            pltpu.VMEM((nb, bs, width), BF16),
            pltpu.VMEM((nb, bs, width), F32),
            pltpu.VMEM((nb, bs, width), F32),
            pltpu.VMEM((nb, bs, lanes), BF16),
            pltpu.VMEM((n_sub, 1, lanes), F32),
            pltpu.VMEM((n_sub, 1, lanes), F32),
            pltpu.VMEM((n_sub, 2 * slots, width // 2), BF16),
            pltpu.VMEM((n_sub, 2 * slots, width // 2), BF16),
            pltpu.VMEM((lanes, width), F32),
            pltpu.VMEM((round_up(nb, 8), width // 2), F32),
            pltpu.VMEM((n_freq, round_up(nb, 8), width // 2), F32),
            dma((9,)),
            dma((n_sub,)), dma((n_sub,)),
            dma((n_sub,)), dma((n_sub,)),
            dma((halves, 2)), dma((halves, 2)),
            dma((n_freq,)), dma((n_freq,)),
        ],
        compiler_params=pltpu.CompilerParams(
            collective_id=0, has_side_effects=True, vmem_limit_bytes=48 * 1024 * 1024
        ),
        name="adjoint_sweeps",
    )(*(pltpu.with_memory_space_constraint(x, pltpu.HBM) for x in (
        response.reshape(nb, bs, width),
        measured.reshape(chans, width),
        sensor_owner.reshape(1, chans),
        sensor_row.reshape(1, chans),
        adj_diag.reshape(nb, 2 * bs, bs),
        adj_off.reshape(nb, nnb, 2 * bs, bs),
        block_cols.T,
        precond.reshape(nb, 2 * bs, bs),
        stiff_deriv,
    )))
    return adjoint[None], gradient.reshape(nb)


def solution(mesh):
    in_specs = (
        P("freq", "sub", None, None),
        P("freq", "sub", None),
        P("sub"),
        P("sub"),
        P("freq", "sub", None, None, None),
        P("freq", "sub", None, None, None, None),
        P("sub", None),
        P("freq", "sub", None, None, None),
        P("sub", None, None),
    )
    out_specs = (P("freq", "sub", None, None), P("sub"))
    body = functools.partial(shards, mesh.shape["sub"], mesh.shape["freq"])
    return jax.shard_map(body, mesh=mesh, in_specs=in_specs, out_specs=out_specs, check_vma=False)
```
